32 devices in a mesh: parts: 2 (over y), row: 8 (over z, x), col: 2 (over core).
Axes of the slice: x: 2, y: 2, z: 4, core: 2. Of those that a mesh axis runs over, the one named last changes fastest.
Arguments:
- cells: bfloat16 [8, 8192], P(None, ('parts', 'row', 'col')), parts along dimension 1, may hold values from -6 to 6
- basis_t: bfloat16 [64, 32, 128], P(('parts', 'row', 'col')), parts along dimension 0, may hold values from -0.5 to 0.5
- near_blocks: bfloat16 [3072, 128, 128], P(('parts', 'row', 'col')), parts along dimension 0, may hold values from -0.0546875 to 0.0546875
- near_owner: int32 [3072, 1], P(('parts', 'row', 'col')), parts along dimension 0, may hold values from 0 to 7; in each aligned block of 96 rows (0 to 95, 96 to 191, ...) at most 24 rows name the same one
- near_col: int32 [3072, 1], P(('parts', 'row', 'col')), parts along dimension 0, may hold values from 0 to 3
- near_row: int32 [3072, 1], P(('parts', 'row', 'col')), parts along dimension 0, may hold values from 0 to 3
- far_row: int32 [4096, 1], P(('parts', 'row', 'col')), parts along dimension 0, may hold values from 0 to 31
- far_col: int32 [4096, 1], P(('parts', 'row', 'col')), parts along dimension 0, may hold values from 0 to 31
- coupling: bfloat16 [4096, 1024], P(('parts', 'row', 'col')), parts along dimension 0, may hold values from -0.09375 to 0.09375
Outputs:
- product: float32 [8, 8192], P(None, ('parts', 'row', 'col')), parts along dimension 1
The draws below stay inside these ranges and needn't reach their ends.
There are 2 independent parts, one for each index of `parts`. The reference program is written for one: setup_inputs(seed, part) draws one part's arguments, and reference() takes and returns one part's arrays. A program takes and returns all parts, laid end to end along the dimension named above; each array names one. Nothing has to cross between parts.
Inputs may be any that keep to these rules, and one draw needn't show every extreme that they name: `near_owner`: in the 96 rows of one device no value appears more than 24 times; in some device one value appears exactly 24 times.
All inputs are finite; a program needn't handle non-finite values.
Results may differ from the reference program's by a relative error of at most 0.0003.
Values may be sent and summed in bfloat16 or wider, within the bound.
No kernel may reach another device: no remote copies, remote signals or barrier semaphores. Data moves between devices by JAX's collectives and lax.ppermute only.
A program may use at most 64 MiB of HBM per device.

```python
import math
import jax
import jax.numpy as jnp
import numpy as np
from jax import lax

B = 128
RK = 32
NRHS = 8
CD = 2
PAIRS = 96
FARS = 128
CL = 4
NC = 32
N = 4096
CAP = 24
PTOT = 1536
FTOT = 2048
N_ROW = 8
N_COL = 2


def plant(values, rng, low, top_value):
    extent = values.shape
    place = [jax.random.randint(jax.random.fold_in(rng, axis), (), 0, extent[axis]) for axis in range(len(extent))]
    values = values.at[tuple(place)].set(low)
    longest = extent.index(max(extent))
    place[longest] = (place[longest] + 1) % extent[longest]
    return values.at[tuple(place)].set(top_value)


def level_of(rng, dims, cuts, low, top_value):
    factor_of = 1.0
    for axis_at, blocks in cuts:
        steps = jax.random.uniform(jax.random.fold_in(jax.random.fold_in(rng, 6), axis_at), (blocks,), jnp.float32, low / len(cuts), top_value / len(cuts))
        factor_of = factor_of * jnp.repeat(jnp.exp(steps), dims[axis_at] // blocks).reshape((-1,) + (1,) * (len(dims) - 1 - axis_at))
    return factor_of


def routed_block(key, own, number, rows, number_of, top, bound, skew):
    ranking = jax.random.permutation(key, number_of)
    crowded, common = shares(number_of, rows * top, bound, skew, True), shares(number_of, rows * top, bound, skew, False)
    places = jnp.arange(number_of)

    def named(sizes, rotation):
        used = int((sizes > 0).sum())
        fixed = max(1, used // 4)
        passed = fixed + (places - fixed + rotation * (used - fixed)) % max(1, number_of - fixed)
        return jnp.zeros((number_of,), jnp.int32).at[ranking[jnp.where(places < fixed, places, passed)]].set(jnp.asarray(sizes, jnp.int32))

    sizes = jnp.where(number % 4 == 0, named(crowded, number // 4), named(common, number - number // 4 - 1))
    mixed = jax.random.permutation(jax.random.fold_in(own, 3), number_of)
    giver, sink = mixed[0:number_of // 2 * 2:2], mixed[1:number_of // 2 * 2:2]
    room = jnp.minimum(sizes[giver] - 1, bound - sizes[sink]) // 2
    room = jnp.where((giver == ranking[0]) | (sink == ranking[0]) | (sizes[sink] == 0), 0, jnp.maximum(room, 0))
    passed = jax.random.randint(jax.random.fold_in(own, 4), (number_of // 2,), 0, 1 << 20) % (room + 1)
    sizes = sizes.at[giver].add(-passed).at[sink].add(passed)
    labels = jnp.searchsorted(jnp.cumsum(sizes), jnp.arange(rows * top), side="right").astype(jnp.int32)
    grid = labels.reshape(top, rows).T
    grid = grid[jax.random.permutation(jax.random.fold_in(own, 1), rows)]
    rotation = jax.random.randint(jax.random.fold_in(own, 2), (rows, 1), 0, top)
    return jnp.take_along_axis(grid, (jnp.arange(top)[None, :] + rotation) % top, axis=1)


def shares(count, total, bound, skew, full):
    loads = [(1 << 20) // math.isqrt(grade ** skew) + 1 for grade in range(1, count + 1)]
    largest = bound if full else min(bound, max(-(-total // count), total * loads[0] // sum(loads)))
    least = 1 if total - largest >= count - 1 else 0
    counts, surplus = [largest] + [least] * (count - 1), total - largest - least * (count - 1)
    while surplus > 0:
        free = [i for i in range(1, count) if counts[i] < largest] or [i for i in range(1, count) if counts[i] < bound]
        whole, left = sum([loads[i] for i in free]), surplus
        for i in free:
            extra = min(bound - counts[i], max(1, left * loads[i] // whole), surplus)
            counts[i] = counts[i] + extra
            surplus = surplus - extra
    return np.array(counts)


def gaussian(rng, dims, deviation, most, cuts=(), held_as=jnp.bfloat16):
    result = jax.random.normal(rng, dims, jnp.float32) * deviation
    if len(cuts) > 0:
        result = level_of(rng, dims, cuts, -0.22, 0.18) * result
    return jnp.clip(result, min=-most, max=most).astype(held_as)


def setup_inputs(seed: int = 0, part: int = 0) -> dict:
    key_of = jax.random.split(jax.random.key(seed), 10)
    part_keys = jax.random.split(jax.random.fold_in(key_of[9], part), 10)
    cells = gaussian(part_keys[0], (NRHS, N), 1.0, 6.0, ((1, 16),))
    basis_t = gaussian(part_keys[1], (NC, RK, B), B ** -0.5, 0.5, ((0, 16),))
    near_blocks = gaussian(part_keys[2], (PTOT, B, B), (B * 2 * PAIRS // CD) ** -0.5, 0.0546875, ((0, 16),))
    near_owner_keys = jax.random.split(jax.random.fold_in(part_keys[3], 1), PTOT // PAIRS)
    near_owner_turns = jax.random.permutation(jax.random.fold_in(part_keys[3], 3), PTOT // PAIRS)
    near_owner = jax.vmap(lambda own, number: routed_block(jax.random.fold_in(part_keys[3], 2), own, number, PAIRS, N_ROW, 1, CAP, 2))(near_owner_keys, near_owner_turns).reshape((PTOT, 1))
    near_col = plant(jax.random.randint(part_keys[4], (PTOT, 1), 0, CL), jax.random.fold_in(part_keys[4], 1), 0, CL - 1).astype(jnp.int32)
    near_row = plant(jax.random.randint(part_keys[5], (PTOT, 1), 0, CL), jax.random.fold_in(part_keys[5], 1), 0, CL - 1).astype(jnp.int32)
    far_row = plant(jax.random.randint(part_keys[6], (FTOT, 1), 0, NC), jax.random.fold_in(part_keys[6], 1), 0, NC - 1).astype(jnp.int32)
    far_col = plant(jax.random.randint(part_keys[7], (FTOT, 1), 0, NC), jax.random.fold_in(part_keys[7], 1), 0, NC - 1).astype(jnp.int32)
    coupling = gaussian(part_keys[8], (FTOT, RK * RK), (RK * 2 * FARS // CD) ** -0.5, 0.09375, ((0, 16),))
    return dict(cells=cells, basis_t=basis_t, near_blocks=near_blocks, near_owner=near_owner, near_col=near_col, near_row=near_row, far_row=far_row, far_col=far_col, coupling=coupling)


def reference(cells, basis_t, near_blocks, near_owner, near_col, near_row, far_row, far_col, coupling):
    highest = lax.Precision.HIGHEST
    field = cells.astype(jnp.float32).reshape(NRHS, NC, B)
    groups = N_ROW * N_COL
    blocks = near_blocks.reshape(groups, PAIRS, B, B)
    row_index = jnp.arange(groups, dtype=jnp.int32) // N_COL
    rows_global = (row_index[:, None] * CL + near_row.reshape(groups, PAIRS)).astype(jnp.int32)
    cols_global = (near_owner.reshape(groups, PAIRS) * CL + near_col.reshape(groups, PAIRS)).astype(jnp.int32)

    def accumulate(total, item):
        block, rows_here, cols_here = item
        matrix = block.astype(jnp.float32)
        col_cells = field[:, cols_here]
        row_cells = field[:, rows_here]
        direct = jnp.einsum('pab,spb->spa', matrix, col_cells, precision=highest)
        mirrored = jnp.einsum('pab,spa->spb', matrix, row_cells, precision=highest)
        total = total.at[:, rows_here].add(direct).at[:, cols_here].add(mirrored)
        return total, None

    near, _ = lax.scan(accumulate, jnp.zeros((NRHS, NC, B), jnp.float32), (blocks, rows_global, cols_global))
    bases = basis_t.astype(jnp.float32)
    moments = jnp.einsum('crb,scb->csr', bases, field, precision=highest)
    matrices = coupling.astype(jnp.float32).reshape(FTOT, RK, RK)
    first = far_row[:, 0]
    second = far_col[:, 0]
    to_first = jnp.einsum('qsk,qrk->qsr', moments[second], matrices, precision=highest)
    to_second = jnp.einsum('qsr,qrk->qsk', moments[first], matrices, precision=highest)
    local_sums = jnp.zeros((NC, NRHS, RK), jnp.float32).at[first].add(to_first).at[second].add(to_second)
    far = jnp.einsum('crb,csr->scb', bases, local_sums, precision=highest)
    return (near + far).reshape(NRHS, NC * B)
```

```python
import jax
import jax.numpy as jnp
from jax import lax
from jax.experimental import pallas as pl
from jax.experimental.pallas import tpu as pltpu
from jax.sharding import PartitionSpec as P

f32 = jnp.float32
bf16 = jnp.bfloat16
LAST = (((1,), (1,)), ((), ()))
PLAIN = (((1,), (0,)), ((), ()))
FIRST = (((0,), (0,)), ((), ()))


def dot(left, right, dims):
    return lax.dot_general(left, right, dims, preferred_element_type=f32)


def halves(value):
    high = value.astype(bf16)
    return high, (value - high.astype(f32)).astype(bf16)


def side_mask(sides, rank):
    row = lax.broadcasted_iota(jnp.int32, (sides, sides * rank), 0)
    lane = lax.broadcasted_iota(jnp.int32, (sides, sides * rank), 1)
    return lane // rank == row


def pack_kernel(cells_ref, basis_ref, out_ref):
    sides = cells_ref.shape[0]
    owned, rank, width = basis_ref.shape
    mask = side_mask(sides, rank)
    high, low = [], []
    for k in range(owned):
        tiled = jnp.concatenate([basis_ref[k]] * sides, axis=0)
        every = dot(cells_ref[:, k * width : (k + 1) * width], tiled, LAST)
        flat = jnp.sum(jnp.where(mask, every, 0.0), axis=0, keepdims=True)
        part = flat.astype(bf16).astype(f32)
        high.append(part)
        low.append(flat - part)
    rest = jnp.zeros((out_ref.shape[1] - sides - 2 * owned, owned * width), f32)
    packed = jnp.concatenate([cells_ref[...].astype(f32)] + high + low + [rest], axis=0)
    packed = packed.astype(bf16)

    def store(d, _):
        out_ref[d] = packed
        return 0

    lax.fori_loop(0, out_ref.shape[0], store, 0, unroll=min(16, out_ref.shape[0]))


def turn_kernel(coupling_ref, by_row_ref, by_col_ref):
    count, size = coupling_ref.shape
    rank = round(size**0.5)
    for t in range(0, size, 128):
        by_row_ref[t : t + 128, :] = coupling_ref[:, t : t + 128].astype(f32).T
    for k in range(rank):
        by_col_ref[k * rank : (k + 1) * rank, :] = by_row_ref[pl.ds(k, rank, stride=rank), :]


def work_kernel(
    index_ref, first_ref, second_ref, every_ref, blocks_ref, by_row_ref, by_col_ref,
    out_ref, row_ref, left_ref, right_ref, to_first_ref, to_second_ref, *, unroll,
):
    devices, lines, lanes = every_ref.shape
    pairs, width, _ = blocks_ref.shape
    sides = out_ref.shape[1]
    count = first_ref.shape[1]
    rank = lanes // sides
    row_clusters = row_ref.shape[0]
    out_ref[...] = jnp.zeros(out_ref.shape, f32)
    row_ref[...] = jnp.zeros(row_ref.shape, f32)
    base = index_ref[2, 0]

    def place(c):
        return c >> 1, pl.ds(pl.multiple_of((c & 1) * width, width), width)

    def group(g, _):
        done = []
        for u in range(unroll):
            p = g * unroll + u
            block = blocks_ref[p]
            i = index_ref[0, p]
            j = index_ref[1, p]
            dj, lj = place(j)
            di, li = place(i + base)
            direct = dot(every_ref[dj, :, lj], block, LAST)
            mirrored = dot(every_ref[di, :, li], block, PLAIN)
            done.append((i, dj, lj, direct, mirrored))
        for i, dj, lj, direct, mirrored in done:
            row_ref[i] += direct[:sides]
            out_ref[dj, :, lj] += mirrored[:sides]
        return 0

    lax.fori_loop(0, pairs // unroll, group, 0)
    for i in range(row_clusters):
        d, l = place(base + i)
        out_ref[d, :, l] += row_ref[i]

    line = lax.broadcasted_iota(jnp.int32, (devices * lines, count), 0)
    hot = []
    for ref in (first_ref, second_ref):
        c = ref[...]
        at = (c >> 1) * lines + sides + (c & 1)
        hot.append(((line == at) | (line == at + 2)).astype(f32).astype(bf16))
    flat = every_ref[...].reshape(devices * lines, lanes)
    left_ref[...] = dot(flat, hot[0], FIRST)
    right_ref[...] = dot(flat, hot[1], FIRST)

    def couple(matrix_ref, moment_ref, result_ref):
        def step(r, sums):
            matrix = matrix_ref[pl.ds(pl.multiple_of(r * rank, rank), rank), :]
            return tuple(
                total + moment_ref[pl.ds(s * rank + r, 1), :] * matrix
                for s, total in enumerate(sums)
            )

        sums = tuple(jnp.zeros((rank, count), f32) for _ in range(sides))
        for s, total in enumerate(lax.fori_loop(0, rank, step, sums, unroll=4)):
            result_ref[s * rank : (s + 1) * rank, :] = total

    couple(by_col_ref, right_ref, to_first_ref)
    couple(by_row_ref, left_ref, to_second_ref)

    line = lax.broadcasted_iota(jnp.int32, (devices * sides, count), 0)
    within = line % sides
    cluster = jnp.where(within < 4, 2 * (line // sides) + within // 2, -1)
    hot_first = (cluster == first_ref[...]).astype(f32).astype(bf16)
    hot_second = (cluster == second_ref[...]).astype(f32).astype(bf16)
    hots = jnp.concatenate([hot_first, hot_first, hot_second, hot_second], axis=1)
    sums = jnp.concatenate(halves(to_first_ref[...]) + halves(to_second_ref[...]), axis=1)
    spread = dot(hots, sums, LAST)
    half = lanes // 2
    odd = lax.broadcasted_iota(jnp.int32, (devices * sides, half), 0) % 2 == 1
    spread = jnp.where(odd, spread[:, half:], spread[:, :half])
    out_ref[:, :, lanes : lanes + half] = spread.reshape(devices, sides, half)


def finish_kernel(parts_ref, basis_ref, out_ref):
    devices, sides, _ = parts_ref.shape
    owned, rank, width = basis_ref.shape
    lanes = owned * width
    half = lanes // 2

    def add(d, total):
        return total + parts_ref[d]

    total = lax.fori_loop(1, devices, add, parts_ref[0], unroll=min(15, devices - 1))
    mask = side_mask(sides, rank)
    for k in range(owned):
        flat = jnp.concatenate(
            [total[2 * k : 2 * k + 1, lanes:], total[2 * k + 1 : 2 * k + 2, lanes:]], axis=1
        )
        high, low = halves(jnp.where(mask, flat, 0.0))
        tiled = jnp.concatenate([basis_ref[k]] * sides, axis=0)
        far = dot(high, tiled, PLAIN) + dot(low, tiled, PLAIN)
        out_ref[:, k * width : (k + 1) * width] = total[:, k * width : (k + 1) * width] + far


def vmem(count):
    return [pl.BlockSpec(memory_space=pltpu.VMEM)] * count


def shards(cells, basis_t, near_blocks, near_owner, near_col, near_row, far_row, far_col, coupling):
    devices = lax.axis_size("row") * lax.axis_size("col")
    sides, lanes = cells.shape
    owned, rank, width = basis_t.shape
    row_clusters = owned * lax.axis_size("col")
    pairs = near_blocks.shape[0]
    count = coupling.shape[0]
    params = pltpu.CompilerParams(vmem_limit_bytes=16 * 1024 * 1024)
    packed = pl.pallas_call(
        pack_kernel,
        out_shape=jax.ShapeDtypeStruct((devices, 16, lanes), bf16),
        in_specs=vmem(2),
        out_specs=pl.BlockSpec(memory_space=pltpu.VMEM),
        compiler_params=params,
        name="pack",
    )(cells, basis_t)
    every = lax.all_to_all(packed, ("row", "col"), split_axis=0, concat_axis=0, tiled=True)
    by_row, by_col = pl.pallas_call(
        turn_kernel,
        out_shape=[jax.ShapeDtypeStruct((rank * rank, count), f32)] * 2,
        in_specs=vmem(1),
        out_specs=vmem(2),
        compiler_params=params,
        cost_estimate=pl.CostEstimate(flops=10**6, bytes_accessed=2 * 10**6, transcendentals=0),
        name="turn",
    )(coupling)
    base = lax.axis_index("row") * row_clusters
    index = jnp.stack(
        [
            near_row[:, 0],
            near_owner[:, 0] * row_clusters + near_col[:, 0],
            jnp.full((pairs,), base, jnp.int32),
        ]
    )
    partial = pl.pallas_call(
        lambda *refs: work_kernel(*refs, unroll=8),
        out_shape=jax.ShapeDtypeStruct((devices, sides, lanes + lanes // 2), f32),
        in_specs=[pl.BlockSpec(memory_space=pltpu.SMEM)] + vmem(6),
        out_specs=pl.BlockSpec(memory_space=pltpu.VMEM),
        scratch_shapes=[
            pltpu.VMEM((row_clusters, sides, width), f32),
            pltpu.VMEM((sides * rank, count), f32),
            pltpu.VMEM((sides * rank, count), f32),
            pltpu.VMEM((sides * rank, count), f32),
            pltpu.VMEM((sides * rank, count), f32),
        ],
        compiler_params=params,
        name="work",
    )(
        index,
        far_row.reshape(1, count),
        far_col.reshape(1, count),
        every,
        near_blocks,
        by_row,
        by_col,
    )
    parts = lax.all_to_all(partial, ("row", "col"), split_axis=0, concat_axis=0, tiled=True)
    return pl.pallas_call(
        finish_kernel,
        out_shape=jax.ShapeDtypeStruct((sides, lanes), f32),
        in_specs=vmem(2),
        out_specs=pl.BlockSpec(memory_space=pltpu.VMEM),
        compiler_params=params,
        name="finish",
    )(parts, basis_t)


def solution(mesh):
    split = ("parts", "row", "col")
    return jax.shard_map(
        shards,
        mesh=mesh,
        in_specs=(
            P(None, split),
            P(split, None, None),
            P(split, None, None),
            P(split, None),
            P(split, None),
            P(split, None),
            P(split, None),
            P(split, None),
            P(split, None),
        ),
        out_specs=P(None, split),
        check_vma=False,
    )
```

```python
import jax
import jax.numpy as jnp
from jax import lax
from jax.experimental import pallas as pl
from jax.experimental.pallas import tpu as pltpu
from jax.sharding import PartitionSpec as P

f32 = jnp.float32
bf16 = jnp.bfloat16
LAST = (((1,), (1,)), ((), ()))
PLAIN = (((1,), (0,)), ((), ()))
FIRST = (((0,), (0,)), ((), ()))
HBM = pl.BlockSpec(memory_space=pltpu.HBM)
VMEM = pl.BlockSpec(memory_space=pltpu.VMEM)
CHUNKS = 4
UNROLL = 8


def dot(left, right, dims):
    return lax.dot_general(left, right, dims, preferred_element_type=f32)


def halves(value):
    high = value.astype(bf16)
    return high, (value - high.astype(f32)).astype(bf16)


def one_hot(match):
    return match.astype(f32).astype(bf16)


def side_mask(sides, rank):
    row = lax.broadcasted_iota(jnp.int32, (sides, sides * rank), 0)
    lane = lax.broadcasted_iota(jnp.int32, (sides, sides * rank), 1)
    return lane // rank == row


def start(source, target, sem):
    copy = pltpu.make_async_copy(source, target, sem)
    copy.start()
    return copy


def in_hbm(array):
    return pltpu.with_memory_space_constraint(array, pltpu.HBM)


def place(cluster, width):
    return cluster >> 1, pl.ds(pl.multiple_of((cluster & 1) * width, width), width)


def pack_kernel(cells_hbm, basis_hbm, out_ref, mine_ref, cells_ref, basis_ref, sems):
    copies = [
        start(cells_hbm, cells_ref, sems.at[0]),
        start(basis_hbm, basis_ref, sems.at[1]),
    ]
    sides = cells_ref.shape[0]
    owned, rank, width = basis_ref.shape
    mask = side_mask(sides, rank)
    for copy in copies:
        copy.wait()
    high, low = [], []
    for k in range(owned):
        tiled = jnp.concatenate([basis_ref[k]] * sides, axis=0)
        every = dot(cells_ref[:, k * width : (k + 1) * width], tiled, LAST)
        flat = jnp.sum(jnp.where(mask, every, 0.0), axis=0, keepdims=True)
        part = flat.astype(bf16).astype(f32)
        high.append(part)
        low.append(flat - part)
    rest = jnp.zeros((mine_ref.shape[0] - sides - 2 * owned, owned * width), f32)
    packed = jnp.concatenate([cells_ref[...].astype(f32)] + high + low + [rest], axis=0)
    packed = packed.astype(bf16)
    mine_ref[...] = packed

    def store(d, _):
        out_ref[d] = packed
        return 0

    lax.fori_loop(0, out_ref.shape[0], store, 0, unroll=min(16, out_ref.shape[0]))


def near_copies(blocks_hbm, blocks_ref, sems, first):
    size = blocks_ref.shape[0] // CHUNKS
    return [
        start(blocks_hbm.at[pl.ds(c * size, size)], blocks_ref.at[pl.ds(c * size, size)], sems.at[first + c])
        for c in range(CHUNKS)
    ]


def near_loop(copies, pairs, body):
    size = pairs // CHUNKS
    for c, copy in enumerate(copies):
        copy.wait()

        def group(g, _, c=c):
            body([c * size + g * UNROLL + u for u in range(UNROLL)])
            return 0

        lax.fori_loop(0, size // UNROLL, group, 0)


def mirror_kernel(
    owner_hbm, col_hbm, row_hbm, first_hbm, second_hbm, coupling_hbm, blocks_hbm, mine_ref, other_ref,
    by_row_ref, by_col_ref, gather_ref, spread_ref, out_ref,
    owner, col, row, far, coupling_ref, blocks_ref, cells_ref, sems,
):
    small = [
        start(owner_hbm, owner, sems.at[0]),
        start(col_hbm, col, sems.at[1]),
        start(row_hbm, row, sems.at[2]),
        start(first_hbm, far.at[0], sems.at[3]),
        start(second_hbm, far.at[1], sems.at[4]),
        start(coupling_hbm, coupling_ref, sems.at[5]),
    ]
    copies = near_copies(blocks_hbm, blocks_ref, sems, 6)
    count, size = coupling_ref.shape
    rank = round(size**0.5)
    devices, sides, _ = out_ref.shape
    lines = gather_ref.shape[0] // devices
    pairs, width, _ = blocks_ref.shape
    row_clusters = 2 * cells_ref.shape[0]
    me = lax.axis_index("col")
    cells_ref[me] = mine_ref[...]
    cells_ref[1 - me] = other_ref[...]
    out_ref[...] = jnp.zeros(out_ref.shape, f32)

    for copy in small:
        copy.wait()
    line = lax.broadcasted_iota(jnp.int32, (devices * lines, count), 0)
    target = lax.broadcasted_iota(jnp.int32, (devices * sides, count), 0)
    within = target % sides
    cluster = jnp.where(within < 4, 2 * (target // sides) + within // 2, -1)
    for n in range(2):
        c = far[n]
        at = (c >> 1) * lines + sides + (c & 1)
        gather_ref[:, n * count : (n + 1) * count] = one_hot((line == at) | (line == at + 2))
        hot = one_hot(cluster == c)
        spread_ref[:, 2 * n * count : (2 * n + 1) * count] = hot
        spread_ref[:, (2 * n + 1) * count : (2 * n + 2) * count] = hot

    for t in range(0, size, 128):
        by_row_ref[t : t + 128, :] = coupling_ref[:, t : t + 128].astype(f32).T
    for k in range(rank):
        by_col_ref[k * rank : (k + 1) * rank, :] = by_row_ref[pl.ds(k, rank, stride=rank), :]

    def body(group):
        done = []
        for p in group:
            d, l = place(row[0, p], width)
            j = owner[0, p] * row_clusters + col[0, p]
            done.append((j, dot(cells_ref[d, :, l], blocks_ref[p], PLAIN)))
        for j, mirrored in done:
            d, l = place(j, width)
            out_ref[d, :, l] += mirrored[:sides]

    near_loop(copies, pairs, body)


def far_kernel(
    every_ref, gather_ref, spread_ref, by_row_ref, by_col_ref, near_ref,
    out_ref, left_ref, right_ref, to_first_ref, to_second_ref,
):
    devices, lines, lanes = every_ref.shape
    sides = out_ref.shape[1]
    count = left_ref.shape[1]
    rank = lanes // sides
    flat = every_ref[...].reshape(devices * lines, lanes)
    moments = dot(flat, gather_ref[...], FIRST)
    left_ref[...] = moments[:, :count]
    right_ref[...] = moments[:, count:]

    def couple(matrix_ref, moment_ref, result_ref):
        def step(r, sums):
            matrix = matrix_ref[pl.ds(pl.multiple_of(r * rank, rank), rank), :]
            return tuple(
                total + moment_ref[pl.ds(s * rank + r, 1), :] * matrix
                for s, total in enumerate(sums)
            )

        sums = tuple(jnp.zeros((rank, count), f32) for _ in range(sides))
        for s, total in enumerate(lax.fori_loop(0, rank, step, sums, unroll=4)):
            result_ref[s * rank : (s + 1) * rank, :] = total

    couple(by_col_ref, right_ref, to_first_ref)
    couple(by_row_ref, left_ref, to_second_ref)
    sums = jnp.concatenate(halves(to_first_ref[...]) + halves(to_second_ref[...]), axis=1)
    spread = dot(spread_ref[...], sums, LAST)
    half = lanes // 2
    odd = lax.broadcasted_iota(jnp.int32, (devices * sides, half), 0) % 2 == 1
    spread = jnp.where(odd, spread[:, half:], spread[:, :half])
    out_ref[:, :, :lanes] = near_ref[...]
    out_ref[:, :, lanes:] = spread.reshape(devices, sides, half)


def direct_kernel(
    owner_hbm, col_hbm, row_hbm, blocks_hbm, every_ref, out_ref, owner, col, row, blocks_ref, sems
):
    small = [
        start(owner_hbm, owner, sems.at[0]),
        start(col_hbm, col, sems.at[1]),
        start(row_hbm, row, sems.at[2]),
    ]
    copies = near_copies(blocks_hbm, blocks_ref, sems, 3)
    pairs, width, _ = blocks_ref.shape
    row_clusters = 2 * out_ref.shape[0]
    sides = out_ref.shape[1]
    out_ref[...] = jnp.zeros(out_ref.shape, f32)
    for copy in small:
        copy.wait()

    def body(group):
        done = []
        for p in group:
            d, l = place(owner[0, p] * row_clusters + col[0, p], width)
            done.append((row[0, p], dot(every_ref[d, :, l], blocks_ref[p], LAST)))
        for i, direct in done:
            d, l = place(i, width)
            out_ref[d, :, l] += direct[:sides]

    near_loop(copies, pairs, body)


def finish_kernel(parts_ref, mine_ref, other_ref, basis_ref, out_ref):
    devices, sides, _ = parts_ref.shape
    owned, rank, width = basis_ref.shape
    lanes = owned * width

    def add(d, total):
        return total + parts_ref[d]

    total = lax.fori_loop(1, devices, add, parts_ref[0], unroll=min(15, devices - 1))
    me = lax.axis_index("col")
    near = total[:, :lanes] + (mine_ref[me] + other_ref[me])
    mask = side_mask(sides, rank)
    for k in range(owned):
        flat = jnp.concatenate(
            [total[2 * k : 2 * k + 1, lanes:], total[2 * k + 1 : 2 * k + 2, lanes:]], axis=1
        )
        high, low = halves(jnp.where(mask, flat, 0.0))
        tiled = jnp.concatenate([basis_ref[k]] * sides, axis=0)
        far = dot(high, tiled, PLAIN) + dot(low, tiled, PLAIN)
        out_ref[:, k * width : (k + 1) * width] = near[:, k * width : (k + 1) * width] + far


def shards(cells, basis_t, near_blocks, near_owner, near_col, near_row, far_row, far_col, coupling):
    everyone = ("row", "col")
    devices = lax.axis_size("row") * lax.axis_size("col")
    sides, lanes = cells.shape
    owned, rank, width = basis_t.shape
    pairs = near_blocks.shape[0]
    count = coupling.shape[0]
    lines = 16
    swap = [(0, 1), (1, 0)]
    params = pltpu.CompilerParams(vmem_limit_bytes=24 * 1024 * 1024)

    def shaped(shape, dtype):
        return jax.ShapeDtypeStruct(shape, dtype)

    def cost(flops, moved):
        return pl.CostEstimate(flops=flops, bytes_accessed=moved, transcendentals=0)

    packed, mine = pl.pallas_call(
        pack_kernel,
        out_shape=[shaped((devices, lines, lanes), bf16), shaped((lines, lanes), bf16)],
        in_specs=[HBM] * 2,
        out_specs=[VMEM] * 2,
        scratch_shapes=[
            pltpu.VMEM(cells.shape, bf16),
            pltpu.VMEM(basis_t.shape, bf16),
            pltpu.SemaphoreType.DMA((2,)),
        ],
        compiler_params=params,
        name="pack",
    )(in_hbm(cells), in_hbm(basis_t))
    every = lax.all_to_all(packed, everyone, split_axis=0, concat_axis=0, tiled=True)
    other = lax.ppermute(mine, "col", swap)
    owner, column, line = [in_hbm(a.reshape(1, pairs)) for a in (near_owner, near_col, near_row)]
    first, second = [in_hbm(a.reshape(1, count)) for a in (far_row, far_col)]
    blocks = in_hbm(near_blocks)
    index_scratch = [pltpu.SMEM((1, pairs), jnp.int32)] * 3
    by_row, by_col, gather, spread, near = pl.pallas_call(
        mirror_kernel,
        out_shape=[
            shaped((rank * rank, count), f32),
            shaped((rank * rank, count), f32),
            shaped((devices * lines, 2 * count), bf16),
            shaped((devices * sides, 4 * count), bf16),
            shaped((devices, sides, lanes), f32),
        ],
        in_specs=[HBM] * 7 + [VMEM] * 2,
        out_specs=[VMEM] * 5,
        scratch_shapes=index_scratch
        + [
            pltpu.VMEM((2, 1, count), jnp.int32),
            pltpu.VMEM(coupling.shape, bf16),
            pltpu.VMEM(near_blocks.shape, bf16),
            pltpu.VMEM((2, lines, lanes), bf16),
            pltpu.SemaphoreType.DMA((6 + CHUNKS,)),
        ],
        compiler_params=params,
        cost_estimate=cost(2 * pairs * 16 * width * width, 10**7),
        name="mirror",
    )(owner, column, line, first, second, in_hbm(coupling), blocks, mine, other)
    partial = pl.pallas_call(
        far_kernel,
        out_shape=shaped((devices, sides, lanes + lanes // 2), f32),
        in_specs=[VMEM] * 6,
        out_specs=VMEM,
        scratch_shapes=[pltpu.VMEM((sides * rank, count), f32)] * 4,
        compiler_params=params,
        name="far",
    )(every, gather, spread, by_row, by_col, near)
    parts = lax.all_to_all(partial, everyone, split_axis=0, concat_axis=0, tiled=True)
    direct = pl.pallas_call(
        direct_kernel,
        out_shape=shaped((2, sides, lanes), f32),
        in_specs=[HBM] * 4 + [VMEM],
        out_specs=VMEM,
        scratch_shapes=index_scratch
        + [pltpu.VMEM(near_blocks.shape, bf16), pltpu.SemaphoreType.DMA((3 + CHUNKS,))],
        compiler_params=params,
        cost_estimate=cost(2 * pairs * 16 * width * width, 10**7),
        name="direct",
    )(owner, column, line, blocks, every)
    others = lax.ppermute(direct, "col", swap)
    return pl.pallas_call(
        finish_kernel,
        out_shape=shaped((sides, lanes), f32),
        in_specs=[VMEM] * 4,
        out_specs=VMEM,
        compiler_params=params,
        name="finish",
    )(parts, direct, others, basis_t)


def solution(mesh):
    split = ("parts", "row", "col")
    return jax.shard_map(
        shards,
        mesh=mesh,
        in_specs=(
            P(None, split),
            P(split, None, None),
            P(split, None, None),
            P(split, None),
            P(split, None),
            P(split, None),
            P(split, None),
            P(split, None),
            P(split, None),
        ),
        out_specs=P(None, split),
        check_vma=False,
    )
```

```python
import jax
import jax.numpy as jnp
from jax import lax
from jax.experimental import pallas as pl
from jax.experimental.pallas import tpu as pltpu
from jax.sharding import Mesh, PartitionSpec as P

f32 = jnp.float32
bf16 = jnp.bfloat16
LAST = (((1,), (1,)), ((), ()))
PLAIN = (((1,), (0,)), ((), ()))
FIRST = (((0,), (0,)), ((), ()))
HBM = pl.BlockSpec(memory_space=pltpu.HBM)
VMEM = pl.BlockSpec(memory_space=pltpu.VMEM)
CHUNKS = 4
UNROLL = 8
GROUP = ("x", "col", "z")


def dot(left, right, dims):
    return lax.dot_general(left, right, dims, preferred_element_type=f32)


def halves(value):
    high = value.astype(bf16)
    return high, (value - high.astype(f32)).astype(bf16)


def one_hot(match):
    return match.astype(f32).astype(bf16)


def side_mask(sides, rank):
    row = lax.broadcasted_iota(jnp.int32, (sides, sides * rank), 0)
    lane = lax.broadcasted_iota(jnp.int32, (sides, sides * rank), 1)
    return lane // rank == row


def start(source, target, sem):
    copy = pltpu.make_async_copy(source, target, sem)
    copy.start()
    return copy


def in_hbm(array):
    return pltpu.with_memory_space_constraint(array, pltpu.HBM)


def slot_of(cluster, inner):
    depth, width = inner
    device = cluster >> 1
    return lax.rem(device, width) * depth + lax.div(device, width)


def each(count, body):
    if count <= 16:
        for d in range(count):
            body(d)
    else:
        pl.loop(0, count)(body)


def pack_kernel(cells_hbm, basis_hbm, out_hbm, mine_ref, cells_ref, basis_ref, out_ref, sems):
    copies = [
        start(cells_hbm, cells_ref, sems.at[0]),
        start(basis_hbm, basis_ref, sems.at[1]),
    ]
    sides = cells_ref.shape[0]
    owned, rank, width = basis_ref.shape
    mask = side_mask(sides, rank)
    for copy in copies:
        copy.wait()
    mine_ref[...] = cells_ref[...]
    cells = cells_ref[...].astype(f32)
    blocks, lines = [], []
    for k in range(owned):
        part = cells[:, k * width : (k + 1) * width]
        blocks += [part[:4], part[4:]]
        tiled = jnp.concatenate([basis_ref[k]] * sides, axis=0)
        every = dot(cells_ref[:, k * width : (k + 1) * width], tiled, LAST)
        flat = jnp.sum(jnp.where(mask, every, 0.0), axis=0, keepdims=True)
        lines += [flat[:, :128], flat[:, 128:]]
    blocks.append(jnp.concatenate(lines, axis=0))

    def store(d):
        for b, block in enumerate(blocks):
            out_ref[d, b] = block

    each(out_ref.shape[0], store)
    start(out_ref, out_hbm, sems.at[0]).wait()


def near_copies(blocks_hbm, blocks_ref, sems, first):
    size = blocks_ref.shape[0] // CHUNKS
    return [
        start(blocks_hbm.at[pl.ds(c * size, size)], blocks_ref.at[pl.ds(c * size, size)], sems.at[first + c])
        for c in range(CHUNKS)
    ]


def near_loop(copies, pairs, body):
    size = pairs // CHUNKS
    for c, copy in enumerate(copies):
        copy.wait()

        def group(g, _, c=c):
            body([c * size + g * UNROLL + u for u in range(UNROLL)])
            return 0

        lax.fori_loop(0, size // UNROLL, group, 0)


def mirror_kernel(
    owner_hbm, col_hbm, row_hbm, first_hbm, second_hbm, coupling_hbm, blocks_hbm, mine_ref, other_ref,
    by_row_ref, by_col_ref, gather_ref, spread_ref, out_ref,
    owner, col, row, far, coupling_ref, blocks_ref, cells_ref, sums_ref, sems, *, inner,
):
    small = [
        start(owner_hbm, owner, sems.at[0]),
        start(col_hbm, col, sems.at[1]),
        start(row_hbm, row, sems.at[2]),
        start(first_hbm, far.at[0], sems.at[3]),
        start(second_hbm, far.at[1], sems.at[4]),
        start(coupling_hbm, coupling_ref, sems.at[5]),
    ]
    copies = near_copies(blocks_hbm, blocks_ref, sems, 6)
    count, size = coupling_ref.shape
    rank = round(size**0.5)
    devices = out_ref.shape[0]
    pairs, width, _ = blocks_ref.shape
    row_clusters = cells_ref.shape[0]
    me = lax.axis_index("col")
    for k in range(2):
        cells_ref[2 * me + k] = mine_ref[:, k * width : (k + 1) * width].astype(f32)
        cells_ref[2 - 2 * me + k] = other_ref[:, k * width : (k + 1) * width].astype(f32)
    sums_ref[...] = jnp.zeros(sums_ref.shape, f32)

    for copy in small:
        copy.wait()
    line = lax.broadcasted_iota(jnp.int32, (4 * devices, count), 0)
    for n in range(2):
        c = far[n]
        at = 4 * slot_of(c, inner) + 2 * (c & 1)
        low, high = line == at, line == at + 1
        for h, match in enumerate((low, high)):
            hot = one_hot(match)
            column = (2 * n + h) * count
            gather_ref[: 4 * devices, column : column + count] = hot
            gather_ref[4 * devices :, column : column + count] = hot
        hot = one_hot(low | high)
        spread_ref[:, 2 * n * count : (2 * n + 1) * count] = hot
        spread_ref[:, (2 * n + 1) * count : (2 * n + 2) * count] = hot

    for t in range(0, size, 128):
        by_row_ref[t : t + 128, :] = coupling_ref[:, t : t + 128].astype(f32).T
    for k in range(rank):
        by_col_ref[k * rank : (k + 1) * rank, :] = by_row_ref[pl.ds(k, rank, stride=rank), :]

    def body(group):
        done = []
        for p in group:
            j = owner[0, p] * row_clusters + col[0, p]
            at = 2 * slot_of(j, inner) + (j & 1)
            done.append((at, dot(cells_ref[row[0, p]].astype(bf16), blocks_ref[p], PLAIN)))
        for at, mirrored in done:
            sums_ref[at] += mirrored

    near_loop(copies, pairs, body)

    def store(d):
        for k in range(2):
            out_ref[d, 2 * k] = sums_ref[2 * d + k, :4, :]
            out_ref[d, 2 * k + 1] = sums_ref[2 * d + k, 4:, :]

    each(devices, store)


def far_kernel(
    every_ref, gather_ref, spread_ref, by_row_ref, by_col_ref, near_ref,
    out_hbm, moment_ref, left_ref, right_ref, to_first_ref, to_second_ref, lines_ref, far_ref, sems,
):
    near = start(near_ref, out_hbm.at[:, pl.ds(0, 4)], sems.at[0])
    devices = every_ref.shape[0]
    size, count = left_ref.shape
    sides = 8
    rank = size // sides

    def load(d):
        moment_ref[pl.ds(4 * d, 4), :] = every_ref[d, 4]

    each(devices, load)
    moments = dot(jnp.concatenate(halves(moment_ref[...]), axis=0), gather_ref[...], FIRST)
    for h in range(2):
        left_ref[h * 128 : (h + 1) * 128, :] = moments[:, h * count : (h + 1) * count]
        right_ref[h * 128 : (h + 1) * 128, :] = moments[:, (2 + h) * count : (3 + h) * count]

    def couple(matrix_ref, moment_ref, result_ref):
        def step(r, sums):
            matrix = matrix_ref[pl.ds(pl.multiple_of(r * rank, rank), rank), :]
            return tuple(
                total + moment_ref[pl.ds(s * rank + r, 1), :] * matrix
                for s, total in enumerate(sums)
            )

        sums = tuple(jnp.zeros((rank, count), f32) for _ in range(sides))
        for s, total in enumerate(lax.fori_loop(0, rank, step, sums, unroll=4)):
            result_ref[s * rank : (s + 1) * rank, :] = total

    couple(by_col_ref, right_ref, to_first_ref)
    couple(by_row_ref, left_ref, to_second_ref)
    sums = jnp.concatenate(halves(to_first_ref[...]) + halves(to_second_ref[...]), axis=1)
    spread = dot(spread_ref[...], sums, LAST)
    odd = lax.broadcasted_iota(jnp.int32, (4 * devices, 128), 0) % 2 == 1
    lines_ref[...] = jnp.where(odd, spread[:, 128:], spread[:, :128])

    def store(d):
        far_ref[d, 0] = lines_ref[pl.ds(4 * d, 4), :]

    each(devices, store)
    far = start(far_ref, out_hbm.at[:, pl.ds(4, 1)], sems.at[1])
    near.wait()
    far.wait()


def direct_kernel(
    owner_hbm, col_hbm, row_hbm, blocks_hbm, every_ref,
    out_ref, owner, col, row, blocks_ref, cells_ref, sems, *, inner,
):
    small = [
        start(owner_hbm, owner, sems.at[0]),
        start(col_hbm, col, sems.at[1]),
        start(row_hbm, row, sems.at[2]),
    ]
    copies = near_copies(blocks_hbm, blocks_ref, sems, 3)
    pairs = blocks_ref.shape[0]
    row_clusters = out_ref.shape[0]
    out_ref[...] = jnp.zeros(out_ref.shape, f32)

    def load(d):
        for k in range(2):
            cells_ref[2 * d + k] = jnp.concatenate([every_ref[d, 2 * k], every_ref[d, 2 * k + 1]], axis=0)

    each(every_ref.shape[0], load)
    for copy in small:
        copy.wait()

    def body(group):
        done = []
        for p in group:
            j = owner[0, p] * row_clusters + col[0, p]
            at = 2 * slot_of(j, inner) + (j & 1)
            done.append((row[0, p], dot(cells_ref[at].astype(bf16), blocks_ref[p], LAST)))
        for i, direct in done:
            out_ref[i] += direct

    near_loop(copies, pairs, body)


def finish_kernel(parts_ref, mine_ref, other_ref, basis_ref, out_ref):
    devices = parts_ref.shape[0]
    owned, rank, width = basis_ref.shape
    sides = out_ref.shape[0]

    def add(d, totals):
        return tuple(total + parts_ref[d, b] for b, total in enumerate(totals))

    first = tuple(parts_ref[0, b] for b in range(5))
    totals = lax.fori_loop(1, devices, add, first, unroll=min(15, devices - 1))
    me = lax.axis_index("col")
    mask = side_mask(sides, rank)
    for k in range(owned):
        near = jnp.concatenate([totals[2 * k], totals[2 * k + 1]], axis=0)
        near = near + (mine_ref[2 * me + k] + other_ref[2 * me + k])
        flat = jnp.concatenate([totals[4][2 * k : 2 * k + 1], totals[4][2 * k + 1 : 2 * k + 2]], axis=1)
        high, low = halves(jnp.where(mask, flat, 0.0))
        tiled = jnp.concatenate([basis_ref[k]] * sides, axis=0)
        far = dot(high, tiled, PLAIN) + dot(low, tiled, PLAIN)
        out_ref[:, k * width : (k + 1) * width] = near + far


def shards(cells, basis_t, near_blocks, near_owner, near_col, near_row, far_row, far_col, coupling):
    depth = lax.axis_size("z")
    inner = (depth, lax.axis_size("x") * lax.axis_size("col"))
    devices = depth * inner[1]
    sides, lanes = cells.shape
    owned, rank, width = basis_t.shape
    row_clusters = owned * lax.axis_size("col")
    pairs = near_blocks.shape[0]
    count = coupling.shape[0]
    swap = [(0, 1), (1, 0)]
    params = pltpu.CompilerParams(vmem_limit_bytes=24 * 1024 * 1024)

    def shaped(shape, dtype):
        return jax.ShapeDtypeStruct(shape, dtype)

    def exchange(blocks):
        return lax.all_to_all(blocks, GROUP, split_axis=0, concat_axis=0, tiled=True)

    near_cost = pl.CostEstimate(
        flops=2 * pairs * sides * width * width, bytes_accessed=10**7, transcendentals=0
    )
    payload = shaped((devices, 5, 4, 128), f32)
    packed, mine = pl.pallas_call(
        pack_kernel,
        out_shape=[payload, shaped(cells.shape, bf16)],
        in_specs=[HBM] * 2,
        out_specs=[HBM, VMEM],
        scratch_shapes=[
            pltpu.VMEM(cells.shape, bf16),
            pltpu.VMEM(basis_t.shape, bf16),
            pltpu.VMEM(payload.shape, f32),
            pltpu.SemaphoreType.DMA((2,)),
        ],
        compiler_params=params,
        name="pack",
    )(in_hbm(cells), in_hbm(basis_t))
    every = exchange(packed)
    other = lax.ppermute(mine, "col", swap)
    owner, column, line = [in_hbm(a.reshape(1, pairs)) for a in (near_owner, near_col, near_row)]
    first, second = [in_hbm(a.reshape(1, count)) for a in (far_row, far_col)]
    blocks = in_hbm(near_blocks)
    index_scratch = [pltpu.SMEM((1, pairs), jnp.int32)] * 3
    by_row, by_col, gather, spread, near = pl.pallas_call(
        lambda *refs: mirror_kernel(*refs, inner=inner),
        out_shape=[
            shaped((rank * rank, count), f32),
            shaped((rank * rank, count), f32),
            shaped((8 * devices, 4 * count), bf16),
            shaped((4 * devices, 4 * count), bf16),
            shaped((devices, 4, 4, 128), f32),
        ],
        in_specs=[HBM] * 7 + [VMEM] * 2,
        out_specs=[VMEM] * 5,
        scratch_shapes=index_scratch
        + [
            pltpu.VMEM((2, 1, count), jnp.int32),
            pltpu.VMEM(coupling.shape, bf16),
            pltpu.VMEM(near_blocks.shape, bf16),
            pltpu.VMEM((row_clusters, sides, width), f32),
            pltpu.VMEM((2 * devices, sides, width), f32),
            pltpu.SemaphoreType.DMA((6 + CHUNKS,)),
        ],
        compiler_params=params,
        cost_estimate=near_cost,
        name="mirror",
    )(owner, column, line, first, second, in_hbm(coupling), blocks, mine, other)
    partial = pl.pallas_call(
        far_kernel,
        out_shape=payload,
        in_specs=[VMEM] * 6,
        out_specs=HBM,
        scratch_shapes=[pltpu.VMEM((4 * devices, 128), f32)]
        + [pltpu.VMEM((sides * rank, count), f32)] * 4
        + [
            pltpu.VMEM((4 * devices, 128), f32),
            pltpu.VMEM((devices, 1, 4, 128), f32),
            pltpu.SemaphoreType.DMA((2,)),
        ],
        compiler_params=params,
        name="far",
    )(every, gather, spread, by_row, by_col, near)
    parts = exchange(partial)
    direct = pl.pallas_call(
        lambda *refs: direct_kernel(*refs, inner=inner),
        out_shape=shaped((row_clusters, sides, width), f32),
        in_specs=[HBM] * 4 + [VMEM],
        out_specs=VMEM,
        scratch_shapes=index_scratch
        + [
            pltpu.VMEM(near_blocks.shape, bf16),
            pltpu.VMEM((2 * devices, sides, width), f32),
            pltpu.SemaphoreType.DMA((3 + CHUNKS,)),
        ],
        compiler_params=params,
        cost_estimate=near_cost,
        name="direct",
    )(owner, column, line, blocks, every)
    others = lax.ppermute(direct, "col", swap)
    return pl.pallas_call(
        finish_kernel,
        out_shape=shaped((sides, lanes), f32),
        in_specs=[VMEM] * 4,
        out_specs=VMEM,
        compiler_params=params,
        name="finish",
    )(parts, direct, others, basis_t)


def solution(mesh):
    parts, rows, cols = mesh.devices.shape
    x = 2 if rows % 2 == 0 else 1
    mesh = Mesh(mesh.devices.reshape(parts, rows // x, x, cols), ("parts", "z", "x", "col"))
    split = ("parts", "z", "x", "col")
    return jax.shard_map(
        shards,
        mesh=mesh,
        in_specs=(
            P(None, split),
            P(split, None, None),
            P(split, None, None),
            P(split, None),
            P(split, None),
            P(split, None),
            P(split, None),
            P(split, None),
            P(split, None),
        ),
        out_specs=P(None, split),
        check_vma=False,
    )
```

```python
import jax
import jax.numpy as jnp
from jax import lax
from jax.experimental import pallas as pl
from jax.experimental.pallas import tpu as pltpu
from jax.sharding import Mesh, PartitionSpec as P

f32 = jnp.float32
bf16 = jnp.bfloat16
LAST = (((1,), (1,)), ((), ()))
PLAIN = (((1,), (0,)), ((), ()))
FIRST = (((0,), (0,)), ((), ()))
HBM = pl.BlockSpec(memory_space=pltpu.HBM)
VMEM = pl.BlockSpec(memory_space=pltpu.VMEM)
CHUNKS = 4
UNROLL = 24
GROUP = ("x", "col", "z")


def dot(left, right, dims):
    return lax.dot_general(left, right, dims, preferred_element_type=f32)


def halves(value):
    high = value.astype(bf16)
    return high, (value - high.astype(f32)).astype(bf16)


def one_hot(match):
    return match.astype(f32).astype(bf16)


def side_mask(sides, rank):
    row = lax.broadcasted_iota(jnp.int32, (sides, sides * rank), 0)
    lane = lax.broadcasted_iota(jnp.int32, (sides, sides * rank), 1)
    return lane // rank == row


def start(source, target, sem):
    copy = pltpu.make_async_copy(source, target, sem)
    copy.start()
    return copy


def in_hbm(array):
    return pltpu.with_memory_space_constraint(array, pltpu.HBM)


def slot_of(cluster, inner):
    depth, width = inner
    device = cluster >> 1
    return lax.rem(device, width) * depth + lax.div(device, width)


def each(count, body):
    if count <= 16:
        for d in range(count):
            body(d)
    else:
        pl.loop(0, count)(body)


def pack_kernel(cells_hbm, basis_hbm, out_hbm, mine_ref, cells_ref, basis_ref, out_ref, sems):
    copies = [
        start(cells_hbm, cells_ref, sems.at[0]),
        start(basis_hbm, basis_ref, sems.at[1]),
    ]
    sides = cells_ref.shape[0]
    owned, rank, width = basis_ref.shape
    mask = side_mask(sides, rank)
    for copy in copies:
        copy.wait()
    mine_ref[...] = cells_ref[...]
    blocks, lines = [], []
    for k in range(owned):
        cells = cells_ref[:, k * width : (k + 1) * width]
        blocks.append(cells)
        tiled = jnp.concatenate([basis_ref[k]] * sides, axis=0)
        every = dot(cells, tiled, LAST)
        flat = jnp.sum(jnp.where(mask, every, 0.0), axis=0, keepdims=True)
        lines += [flat[:, :128], flat[:, 128:]]
    moments = jnp.concatenate(lines, axis=0)
    high = moments.astype(bf16).astype(f32)
    blocks.append(jnp.concatenate([high, moments - high], axis=0).astype(bf16))

    def store(d):
        for b, block in enumerate(blocks):
            out_ref[d, b] = block

    each(out_ref.shape[0], store)
    start(out_ref, out_hbm, sems.at[0]).wait()


def near_copies(blocks_hbm, blocks_ref, sems, first):
    size = blocks_ref.shape[0] // CHUNKS
    return [
        start(blocks_hbm.at[pl.ds(c * size, size)], blocks_ref.at[pl.ds(c * size, size)], sems.at[first + c])
        for c in range(CHUNKS)
    ]


def near_loop(copies, pairs, body):
    size = pairs // CHUNKS
    for c, copy in enumerate(copies):
        copy.wait()

        def group(g, _, c=c):
            body([c * size + g * UNROLL + u for u in range(UNROLL)])
            return 0

        lax.fori_loop(0, size // UNROLL, group, 0)


def mirror_kernel(
    owner_hbm, col_hbm, row_hbm, first_hbm, second_hbm, coupling_hbm, blocks_hbm, mine_ref, other_ref,
    by_row_ref, by_col_ref, gather_ref, spread_ref, out_ref,
    owner, col, row, far, coupling_ref, blocks_ref, cells_ref, sums_ref, sems, *, inner,
):
    small = [
        start(owner_hbm, owner, sems.at[0]),
        start(col_hbm, col, sems.at[1]),
        start(row_hbm, row, sems.at[2]),
        start(first_hbm, far.at[0], sems.at[3]),
        start(second_hbm, far.at[1], sems.at[4]),
        start(coupling_hbm, coupling_ref, sems.at[5]),
    ]
    copies = near_copies(blocks_hbm, blocks_ref, sems, 6)
    count, size = coupling_ref.shape
    rank = round(size**0.5)
    devices = out_ref.shape[0]
    pairs, width, _ = blocks_ref.shape
    row_clusters = cells_ref.shape[0]
    me = lax.axis_index("col")
    for k in range(2):
        cells_ref[2 * me + k] = mine_ref[:, k * width : (k + 1) * width].astype(f32)
        cells_ref[2 - 2 * me + k] = other_ref[:, k * width : (k + 1) * width].astype(f32)
    sums_ref[...] = jnp.zeros(sums_ref.shape, f32)

    for copy in small:
        copy.wait()
    source = lax.broadcasted_iota(jnp.int32, (8 * devices, count), 0)
    target = lax.broadcasted_iota(jnp.int32, (4 * devices, count), 0)
    for n in range(2):
        c = far[n]
        slot, k = slot_of(c, inner), c & 1
        for h in range(2):
            at = 8 * slot + 2 * k + h
            hot = one_hot((source == at) | (source == at + 4))
            gather_ref[:, (2 * n + h) * count : (2 * n + h + 1) * count] = hot
        at = 4 * slot + 2 * k
        hot = ((target == at) | (target == at + 1)).astype(f32).T.astype(bf16)
        spread_ref[2 * n * count : (2 * n + 1) * count, :] = hot
        spread_ref[(2 * n + 1) * count : (2 * n + 2) * count, :] = hot

    for t in range(0, size, 128):
        by_row_ref[t : t + 128, :] = coupling_ref[:, t : t + 128].astype(f32).T
    for k in range(rank):
        by_col_ref[k * rank : (k + 1) * rank, :] = by_row_ref[pl.ds(k, rank, stride=rank), :]

    def body(group):
        done = []
        for p in group:
            j = owner[0, p] * row_clusters + col[0, p]
            at = 2 * slot_of(j, inner) + (j & 1)
            done.append((at, dot(cells_ref[row[0, p]].astype(bf16), blocks_ref[p], PLAIN)))
        for at, mirrored in done:
            sums_ref[at] += mirrored

    near_loop(copies, pairs, body)

    def store(d):
        for k in range(2):
            out_ref[d, 2 * k] = sums_ref[2 * d + k, :4, :]
            out_ref[d, 2 * k + 1] = sums_ref[2 * d + k, 4:, :]

    each(devices, store)


def far_kernel(
    every_ref, gather_ref, spread_ref, by_row_ref, by_col_ref, near_ref,
    out_hbm, left_ref, right_ref, lines_ref, far_ref, sems,
):
    near = start(near_ref, out_hbm.at[:, pl.ds(0, 4)], sems.at[0])
    devices = every_ref.shape[0]
    size, count = left_ref.shape
    sides = 8
    rank = size // sides

    lines = every_ref[:, 2].astype(f32).reshape(8 * devices, 128).astype(bf16)
    moments = dot(lines, gather_ref[...], FIRST)
    for h in range(2):
        left_ref[h * 128 : (h + 1) * 128, :] = moments[:, h * count : (h + 1) * count]
        right_ref[h * 128 : (h + 1) * 128, :] = moments[:, (2 + h) * count : (3 + h) * count]

    lines = []
    for h in range(2):
        total = 0.0
        for n, (matrix_ref, source_ref) in enumerate(((by_col_ref, right_ref), (by_row_ref, left_ref))):
            sums = [jnp.zeros((rank, count), f32) for _ in range(sides // 2)]
            for r in range(rank):
                matrix = matrix_ref[r * rank : (r + 1) * rank, :]
                for s in range(sides // 2):
                    at = h * 128 + s * rank + r
                    sums[s] = sums[s] + source_ref[at : at + 1, :] * matrix
            pair = jnp.concatenate(halves(jnp.concatenate(sums, axis=0)), axis=1)
            total = total + dot(pair, spread_ref[2 * n * count : (2 * n + 2) * count, :], PLAIN)
        lines.append(total)
    odd = lax.broadcasted_iota(jnp.int32, (128, 4 * devices), 1) % 2 == 1
    lines_ref[...] = jnp.where(odd, lines[1], lines[0]).T

    def store(d):
        far_ref[d, 0] = lines_ref[pl.ds(4 * d, 4), :]

    each(devices, store)
    far = start(far_ref, out_hbm.at[:, pl.ds(4, 1)], sems.at[1])
    near.wait()
    far.wait()


def direct_kernel(
    owner_hbm, col_hbm, row_hbm, blocks_hbm, every_ref,
    out_ref, owner, col, row, blocks_ref, sems, *, inner,
):
    small = [
        start(owner_hbm, owner, sems.at[0]),
        start(col_hbm, col, sems.at[1]),
        start(row_hbm, row, sems.at[2]),
    ]
    copies = near_copies(blocks_hbm, blocks_ref, sems, 3)
    pairs = blocks_ref.shape[0]
    row_clusters = out_ref.shape[0]
    out_ref[...] = jnp.zeros(out_ref.shape, f32)

    for copy in small:
        copy.wait()

    def body(group):
        done = []
        for p in group:
            j = owner[0, p] * row_clusters + col[0, p]
            cells = every_ref[slot_of(j, inner), j & 1]
            done.append((row[0, p], dot(cells, blocks_ref[p], LAST)))
        for i, direct in done:
            out_ref[i] += direct

    near_loop(copies, pairs, body)


def finish_kernel(parts_ref, mine_ref, other_ref, basis_ref, out_ref):
    devices = parts_ref.shape[0]
    owned, rank, width = basis_ref.shape
    sides = out_ref.shape[0]

    def add(d, totals):
        return tuple(total + parts_ref[d, b] for b, total in enumerate(totals))

    first = tuple(parts_ref[0, b] for b in range(5))
    totals = lax.fori_loop(1, devices, add, first, unroll=min(15, devices - 1))
    me = lax.axis_index("col")
    mask = side_mask(sides, rank)
    for k in range(owned):
        near = jnp.concatenate([totals[2 * k], totals[2 * k + 1]], axis=0)
        near = near + (mine_ref[2 * me + k] + other_ref[2 * me + k])
        flat = jnp.concatenate([totals[4][2 * k : 2 * k + 1], totals[4][2 * k + 1 : 2 * k + 2]], axis=1)
        high, low = halves(jnp.where(mask, flat, 0.0))
        tiled = jnp.concatenate([basis_ref[k]] * sides, axis=0)
        far = dot(high, tiled, PLAIN) + dot(low, tiled, PLAIN)
        out_ref[:, k * width : (k + 1) * width] = near + far


def shards(cells, basis_t, near_blocks, near_owner, near_col, near_row, far_row, far_col, coupling):
    depth = lax.axis_size("z")
    inner = (depth, lax.axis_size("x") * lax.axis_size("col"))
    devices = depth * inner[1]
    sides, lanes = cells.shape
    owned, rank, width = basis_t.shape
    row_clusters = owned * lax.axis_size("col")
    pairs = near_blocks.shape[0]
    count = coupling.shape[0]
    swap = [(0, 1), (1, 0)]
    params = pltpu.CompilerParams(vmem_limit_bytes=24 * 1024 * 1024)

    def shaped(shape, dtype):
        return jax.ShapeDtypeStruct(shape, dtype)

    def exchange(blocks):
        return lax.all_to_all(blocks, GROUP, split_axis=0, concat_axis=0, tiled=True)

    near_cost = pl.CostEstimate(
        flops=2 * pairs * sides * width * width, bytes_accessed=10**7, transcendentals=0
    )
    payload = shaped((devices, 3, sides, 128), bf16)
    packed, mine = pl.pallas_call(
        pack_kernel,
        out_shape=[payload, shaped(cells.shape, bf16)],
        in_specs=[HBM] * 2,
        out_specs=[HBM, VMEM],
        scratch_shapes=[
            pltpu.VMEM(cells.shape, bf16),
            pltpu.VMEM(basis_t.shape, bf16),
            pltpu.VMEM(payload.shape, bf16),
            pltpu.SemaphoreType.DMA((2,)),
        ],
        compiler_params=params,
        name="pack",
    )(in_hbm(cells), in_hbm(basis_t))
    every = exchange(packed)
    other = lax.ppermute(mine, "col", swap)
    owner, column, line = [in_hbm(a.reshape(1, pairs)) for a in (near_owner, near_col, near_row)]
    first, second = [in_hbm(a.reshape(1, count)) for a in (far_row, far_col)]
    blocks = in_hbm(near_blocks)
    index_scratch = [pltpu.SMEM((1, pairs), jnp.int32)] * 3
    by_row, by_col, gather, spread, near = pl.pallas_call(
        lambda *refs: mirror_kernel(*refs, inner=inner),
        out_shape=[
            shaped((rank * rank, count), f32),
            shaped((rank * rank, count), f32),
            shaped((8 * devices, 4 * count), bf16),
            shaped((4 * count, 4 * devices), bf16),
            shaped((devices, 4, 4, 128), f32),
        ],
        in_specs=[HBM] * 7 + [VMEM] * 2,
        out_specs=[VMEM] * 5,
        scratch_shapes=index_scratch
        + [
            pltpu.VMEM((2, 1, count), jnp.int32),
            pltpu.VMEM(coupling.shape, bf16),
            pltpu.VMEM(near_blocks.shape, bf16),
            pltpu.VMEM((row_clusters, sides, width), f32),
            pltpu.VMEM((2 * devices, sides, width), f32),
            pltpu.SemaphoreType.DMA((6 + CHUNKS,)),
        ],
        compiler_params=params,
        cost_estimate=near_cost,
        name="mirror",
    )(owner, column, line, first, second, in_hbm(coupling), blocks, mine, other)
    partial = pl.pallas_call(
        far_kernel,
        out_shape=shaped((devices, 5, 4, 128), f32),
        in_specs=[VMEM] * 6,
        out_specs=HBM,
        scratch_shapes=[pltpu.VMEM((sides * rank, count), f32)] * 2
        + [
            pltpu.VMEM((4 * devices, 128), f32),
            pltpu.VMEM((devices, 1, 4, 128), f32),
            pltpu.SemaphoreType.DMA((2,)),
        ],
        compiler_params=params,
        name="far",
    )(every, gather, spread, by_row, by_col, near)
    parts = exchange(partial)
    direct = pl.pallas_call(
        lambda *refs: direct_kernel(*refs, inner=inner),
        out_shape=shaped((row_clusters, sides, width), f32),
        in_specs=[HBM] * 4 + [VMEM],
        out_specs=VMEM,
        scratch_shapes=index_scratch
        + [
            pltpu.VMEM(near_blocks.shape, bf16),
            pltpu.SemaphoreType.DMA((3 + CHUNKS,)),
        ],
        compiler_params=params,
        cost_estimate=near_cost,
        name="direct",
    )(owner, column, line, blocks, every)
    others = lax.ppermute(direct, "col", swap)
    return pl.pallas_call(
        finish_kernel,
        out_shape=shaped((sides, lanes), f32),
        in_specs=[VMEM] * 4,
        out_specs=VMEM,
        compiler_params=params,
        name="finish",
    )(parts, direct, others, basis_t)


def solution(mesh):
    parts, rows, cols = mesh.devices.shape
    x = 2 if rows % 2 == 0 else 1
    mesh = Mesh(mesh.devices.reshape(parts, rows // x, x, cols), ("parts", "z", "x", "col"))
    split = ("parts", "z", "x", "col")
    return jax.shard_map(
        shards,
        mesh=mesh,
        in_specs=(
            P(None, split),
            P(split, None, None),
            P(split, None, None),
            P(split, None),
            P(split, None),
            P(split, None),
            P(split, None),
            P(split, None),
            P(split, None),
        ),
        out_specs=P(None, split),
        check_vma=False,
    )
```

```python
import jax
import jax.numpy as jnp
from jax import lax
from jax.experimental import pallas as pl
from jax.experimental.pallas import tpu as pltpu
from jax.sharding import Mesh, PartitionSpec as P

f32 = jnp.float32
bf16 = jnp.bfloat16
LAST = (((1,), (1,)), ((), ()))
PLAIN = (((1,), (0,)), ((), ()))
FIRST = (((0,), (0,)), ((), ()))
HBM = pl.BlockSpec(memory_space=pltpu.HBM)
VMEM = pl.BlockSpec(memory_space=pltpu.VMEM)
CHUNKS = 4
UNROLL = 24
EARLY = 2
GROUP = ("x", "col", "z")


def dot(left, right, dims):
    return lax.dot_general(left, right, dims, preferred_element_type=f32)


def halves(value):
    high = value.astype(bf16)
    return high, (value - high.astype(f32)).astype(bf16)


def one_hot(match):
    return match.astype(f32).astype(bf16)


def side_mask(sides, rank):
    row = lax.broadcasted_iota(jnp.int32, (sides, sides * rank), 0)
    lane = lax.broadcasted_iota(jnp.int32, (sides, sides * rank), 1)
    return lane // rank == row


def start(source, target, sem):
    copy = pltpu.make_async_copy(source, target, sem)
    copy.start()
    return copy


def in_hbm(array):
    return pltpu.with_memory_space_constraint(array, pltpu.HBM)


def slot_of(cluster, inner):
    depth, width = inner
    device = cluster >> 1
    return lax.rem(device, 2 * width) * depth + lax.div(device, 2 * width)


def each(count, body):
    if count <= 16:
        for d in range(count):
            body(d)
    else:
        pl.loop(0, count)(body)


def pack_kernel(
    cells_hbm, basis_hbm, first_hbm, second_hbm, coupling_hbm, blocks_hbm,
    out_hbm, mine_ref, far_ref, coupling_ref, early_ref,
    cells_ref, basis_ref, out_ref, sems, *, inner,
):
    copies = [
        start(cells_hbm, cells_ref, sems.at[0]),
        start(basis_hbm, basis_ref, sems.at[1]),
    ]
    ahead = [
        start(first_hbm, far_ref.at[0], sems.at[2]),
        start(second_hbm, far_ref.at[1], sems.at[3]),
        start(coupling_hbm, coupling_ref, sems.at[4]),
        start(blocks_hbm.at[pl.ds(0, early_ref.shape[0])], early_ref, sems.at[5]),
    ]
    sides = cells_ref.shape[0]
    owned, rank, width = basis_ref.shape
    mask = side_mask(sides, rank)
    for copy in copies:
        copy.wait()
    mine_ref[...] = cells_ref[...]
    blocks, lines = [], []
    for k in range(owned):
        cells = cells_ref[:, k * width : (k + 1) * width]
        blocks.append(cells.astype(f32))
        tiled = jnp.concatenate([basis_ref[k]] * sides, axis=0)
        every = dot(cells, tiled, LAST)
        flat = jnp.sum(jnp.where(mask, every, 0.0), axis=0, keepdims=True)
        lines += [flat[:, :128], flat[:, 128:]]
    moments = jnp.concatenate(lines, axis=0)
    high = moments.astype(bf16).astype(f32)
    moments = jnp.concatenate([high, moments - high], axis=0).astype(bf16)
    for c in range(2):
        half = jnp.concatenate([block[4 * c : 4 * c + 4] for block in blocks], axis=0).astype(bf16)
        for x in range(inner[1]):

            def store(z, c=c, x=x, half=half):
                d = (2 * x + c) * inner[0] + z
                out_ref[d, 0] = half
                out_ref[d, 1] = moments

            each(inner[0], store)
    start(out_ref, out_hbm, sems.at[0]).wait()
    for copy in ahead:
        copy.wait()


def near_copies(blocks_hbm, blocks_ref, sems, first, chunks):
    size = blocks_hbm.shape[0] // CHUNKS
    skipped = CHUNKS - chunks
    return [
        start(
            blocks_hbm.at[pl.ds((skipped + c) * size, size)],
            blocks_ref.at[pl.ds(c * size, size)],
            sems.at[first + c],
        )
        for c in range(chunks)
    ]


def near_loop(first, size, body):
    def group(g, _):
        body([first + g * UNROLL + u for u in range(UNROLL)])
        return 0

    lax.fori_loop(0, size // UNROLL, group, 0)


def mirror_kernel(
    owner_hbm, col_hbm, row_hbm, blocks_hbm, far, coupling_ref, early_ref, mine_ref, other_ref,
    by_row_ref, by_col_ref, gather_ref, spread_ref, keep_ref, give_ref,
    owner, col, row, blocks_ref, cells_ref, sums_ref, sems, *, inner,
):
    small = [
        start(owner_hbm, owner, sems.at[0]),
        start(col_hbm, col, sems.at[1]),
        start(row_hbm, row, sems.at[2]),
    ]
    copies = near_copies(blocks_hbm, blocks_ref, sems, 3, CHUNKS - EARLY)
    count, size = coupling_ref.shape
    rank = round(size**0.5)
    devices = keep_ref.shape[0]
    early, width, _ = early_ref.shape
    chunk = early // EARLY
    row_clusters = cells_ref.shape[0]
    me = lax.axis_index("col")
    for k in range(2):
        cells_ref[2 * me + k] = mine_ref[:, k * width : (k + 1) * width].astype(f32)
        cells_ref[2 - 2 * me + k] = other_ref[:, k * width : (k + 1) * width].astype(f32)
    sums_ref[...] = jnp.zeros(sums_ref.shape, f32)

    source = lax.broadcasted_iota(jnp.int32, (8 * devices, count), 0)
    target = lax.broadcasted_iota(jnp.int32, (4 * devices, count), 0)
    for n in range(2):
        c = far[n]
        slot, k = slot_of(c, inner), c & 1
        for h in range(2):
            at = 8 * slot + 2 * k + h
            hot = one_hot((source == at) | (source == at + 4))
            gather_ref[:, (2 * n + h) * count : (2 * n + h + 1) * count] = hot
        at = 4 * slot + 2 * k
        hot = ((target == at) | (target == at + 1)).astype(f32).T.astype(bf16)
        spread_ref[2 * n * count : (2 * n + 1) * count, :] = hot
        spread_ref[(2 * n + 1) * count : (2 * n + 2) * count, :] = hot

    for t in range(0, size, 128):
        by_row_ref[t : t + 128, :] = coupling_ref[:, t : t + 128].astype(f32).T
    for k in range(rank):
        by_col_ref[k * rank : (k + 1) * rank, :] = by_row_ref[pl.ds(k, rank, stride=rank), :]

    def multiply(source_ref, first):
        def body(group):
            done = []
            for p in group:
                j = owner[0, p] * row_clusters + col[0, p]
                at = 2 * slot_of(j, inner) + (j & 1)
                done.append((at, dot(cells_ref[row[0, p]].astype(bf16), source_ref[p - first], PLAIN)))
            for at, mirrored in done:
                sums_ref[at] += mirrored

        return body

    for copy in small:
        copy.wait()
    near_loop(0, early, multiply(early_ref, 0))
    for c, copy in enumerate(copies):
        copy.wait()
        near_loop(early + c * chunk, chunk, multiply(blocks_ref, early))

    def store(d):
        for k in range(2):
            keep_ref[d, k] = sums_ref[2 * d + k, pl.ds(4 * me, 4), :]
            give_ref[d, k] = sums_ref[2 * d + k, pl.ds(4 - 4 * me, 4), :]

    each(devices, store)


def far_kernel(
    every_ref, gather_ref, spread_ref, by_row_ref, by_col_ref, keep_ref, got_ref,
    out_hbm, near_ref, left_ref, right_ref, lines_ref, far_ref, sems,
):
    near_ref[...] = keep_ref[...] + got_ref[...]
    near = start(near_ref, out_hbm.at[:, pl.ds(0, 2)], sems.at[0])
    devices = every_ref.shape[0]
    size, count = left_ref.shape
    sides = 8
    rank = size // sides

    lines = every_ref[:, 1].astype(f32).reshape(8 * devices, 128).astype(bf16)
    moments = dot(lines, gather_ref[...], FIRST)
    for h in range(2):
        left_ref[h * 128 : (h + 1) * 128, :] = moments[:, h * count : (h + 1) * count]
        right_ref[h * 128 : (h + 1) * 128, :] = moments[:, (2 + h) * count : (3 + h) * count]

    lines = []
    for h in range(2):
        total = 0.0
        for n, (matrix_ref, source_ref) in enumerate(((by_col_ref, right_ref), (by_row_ref, left_ref))):
            sums = [jnp.zeros((rank, count), f32) for _ in range(sides // 2)]
            for r in range(rank):
                matrix = matrix_ref[r * rank : (r + 1) * rank, :]
                for s in range(sides // 2):
                    at = h * 128 + s * rank + r
                    sums[s] = sums[s] + source_ref[at : at + 1, :] * matrix
            pair = jnp.concatenate(halves(jnp.concatenate(sums, axis=0)), axis=1)
            total = total + dot(pair, spread_ref[2 * n * count : (2 * n + 2) * count, :], PLAIN)
        lines.append(total)
    odd = lax.broadcasted_iota(jnp.int32, (128, 4 * devices), 1) % 2 == 1
    lines_ref[...] = jnp.where(odd, lines[1], lines[0]).T

    def store(d):
        far_ref[d, 0] = lines_ref[pl.ds(4 * d, 4), :]

    each(devices, store)
    far = start(far_ref, out_hbm.at[:, pl.ds(2, 1)], sems.at[1])
    near.wait()
    far.wait()


def direct_kernel(
    owner_hbm, col_hbm, row_hbm, blocks_hbm, every_ref, others_ref,
    out_ref, owner, col, row, blocks_ref, cells_ref, sems, *, inner,
):
    small = [
        start(owner_hbm, owner, sems.at[0]),
        start(col_hbm, col, sems.at[1]),
        start(row_hbm, row, sems.at[2]),
    ]
    copies = near_copies(blocks_hbm, blocks_ref, sems, 3, CHUNKS)
    chunk = blocks_ref.shape[0] // CHUNKS
    row_clusters = out_ref.shape[0]
    out_ref[...] = jnp.zeros(out_ref.shape, f32)
    me = lax.axis_index("col")

    def load(d):
        mine, other = every_ref[d, 0].astype(f32), others_ref[d, 0].astype(f32)
        first, second = jnp.where(me == 0, mine, other), jnp.where(me == 0, other, mine)
        for k in range(2):
            cells_ref[d, k] = jnp.concatenate([first[4 * k : 4 * k + 4], second[4 * k : 4 * k + 4]], axis=0)

    each(every_ref.shape[0], load)
    for copy in small:
        copy.wait()

    def body(group):
        done = []
        for p in group:
            j = owner[0, p] * row_clusters + col[0, p]
            cells = cells_ref[slot_of(j, inner), j & 1].astype(bf16)
            done.append((row[0, p], dot(cells, blocks_ref[p], LAST)))
        for i, direct in done:
            out_ref[i] += direct

    for c, copy in enumerate(copies):
        copy.wait()
        near_loop(c * chunk, chunk, body)


def finish_kernel(parts_ref, mine_ref, other_ref, basis_ref, out_ref, *, inner):
    owned, rank, width = basis_ref.shape
    sides = out_ref.shape[0]
    depth = inner[0]
    near, far = [], jnp.zeros((4, 128), f32)
    for c in range(2):
        totals = (jnp.zeros((4, 128), f32), jnp.zeros((4, 128), f32), far)
        for x in range(inner[1]):

            def add(z, totals, first=(2 * x + c) * depth):
                return tuple(total + parts_ref[first + z, b] for b, total in enumerate(totals))

            totals = lax.fori_loop(0, depth, add, totals, unroll=min(8, depth))
        near.append(totals[:2])
        far = totals[2]
    me = lax.axis_index("col")
    mask = side_mask(sides, rank)
    for k in range(owned):
        total = jnp.concatenate([near[0][k], near[1][k]], axis=0)
        total = total + (mine_ref[2 * me + k] + other_ref[2 * me + k])
        flat = jnp.concatenate([far[2 * k : 2 * k + 1], far[2 * k + 1 : 2 * k + 2]], axis=1)
        high, low = halves(jnp.where(mask, flat, 0.0))
        tiled = jnp.concatenate([basis_ref[k]] * sides, axis=0)
        total = total + (dot(high, tiled, PLAIN) + dot(low, tiled, PLAIN))
        out_ref[:, k * width : (k + 1) * width] = total


def shards(cells, basis_t, near_blocks, near_owner, near_col, near_row, far_row, far_col, coupling):
    depth = lax.axis_size("z")
    inner = (depth, lax.axis_size("x"))
    devices = 2 * depth * inner[1]
    sides, lanes = cells.shape
    owned, rank, width = basis_t.shape
    row_clusters = owned * lax.axis_size("col")
    pairs = near_blocks.shape[0]
    count = coupling.shape[0]
    swap = [(0, 1), (1, 0)]
    params = pltpu.CompilerParams(vmem_limit_bytes=24 * 1024 * 1024)

    def shaped(shape, dtype):
        return jax.ShapeDtypeStruct(shape, dtype)

    def exchange(blocks):
        return lax.all_to_all(blocks, GROUP, split_axis=0, concat_axis=0, tiled=True)

    near_cost = pl.CostEstimate(
        flops=2 * pairs * sides * width * width, bytes_accessed=10**7, transcendentals=0
    )
    payload = shaped((devices, 2, sides, 128), bf16)
    owner, column, line = [in_hbm(a.reshape(1, pairs)) for a in (near_owner, near_col, near_row)]
    first, second = [in_hbm(a.reshape(1, count)) for a in (far_row, far_col)]
    blocks = in_hbm(near_blocks)
    early = EARLY * (pairs // CHUNKS)
    packed, mine, far, couplings, early_blocks = pl.pallas_call(
        lambda *refs: pack_kernel(*refs, inner=inner),
        out_shape=[
            payload,
            shaped(cells.shape, bf16),
            shaped((2, 1, count), jnp.int32),
            shaped(coupling.shape, bf16),
            shaped((early,) + near_blocks.shape[1:], bf16),
        ],
        in_specs=[HBM] * 6,
        out_specs=[HBM] + [VMEM] * 4,
        scratch_shapes=[
            pltpu.VMEM(cells.shape, bf16),
            pltpu.VMEM(basis_t.shape, bf16),
            pltpu.VMEM(payload.shape, bf16),
            pltpu.SemaphoreType.DMA((6,)),
        ],
        compiler_params=params,
        name="pack",
    )(in_hbm(cells), in_hbm(basis_t), first, second, in_hbm(coupling), blocks)
    every = exchange(packed)
    other = lax.ppermute(mine, "col", swap)
    index_scratch = [pltpu.SMEM((1, pairs), jnp.int32)] * 3
    by_row, by_col, gather, spread, keep, give = pl.pallas_call(
        lambda *refs: mirror_kernel(*refs, inner=inner),
        out_shape=[
            shaped((rank * rank, count), f32),
            shaped((rank * rank, count), f32),
            shaped((8 * devices, 4 * count), bf16),
            shaped((4 * count, 4 * devices), bf16),
            shaped((devices, 2, 4, 128), f32),
            shaped((devices, 2, 4, 128), f32),
        ],
        in_specs=[HBM] * 4 + [VMEM] * 5,
        out_specs=[VMEM] * 6,
        scratch_shapes=index_scratch
        + [
            pltpu.VMEM((pairs - early,) + near_blocks.shape[1:], bf16),
            pltpu.VMEM((row_clusters, sides, width), f32),
            pltpu.VMEM((2 * devices, sides, width), f32),
            pltpu.SemaphoreType.DMA((3 + CHUNKS,)),
        ],
        compiler_params=params,
        cost_estimate=near_cost,
        name="mirror",
    )(owner, column, line, blocks, far, couplings, early_blocks, mine, other)
    got = lax.ppermute(give, "col", swap)
    partial = pl.pallas_call(
        far_kernel,
        out_shape=shaped((devices, 3, 4, 128), f32),
        in_specs=[VMEM] * 7,
        out_specs=HBM,
        scratch_shapes=[pltpu.VMEM(keep.shape, f32)]
        + [pltpu.VMEM((sides * rank, count), f32)] * 2
        + [
            pltpu.VMEM((4 * devices, 128), f32),
            pltpu.VMEM((devices, 1, 4, 128), f32),
            pltpu.SemaphoreType.DMA((2,)),
        ],
        compiler_params=params,
        name="far",
    )(every, gather, spread, by_row, by_col, keep, got)
    parts = exchange(partial)
    every_other = lax.ppermute(every, "col", swap)
    direct = pl.pallas_call(
        lambda *refs: direct_kernel(*refs, inner=inner),
        out_shape=shaped((row_clusters, sides, width), f32),
        in_specs=[HBM] * 4 + [VMEM] * 2,
        out_specs=VMEM,
        scratch_shapes=index_scratch
        + [
            pltpu.VMEM(near_blocks.shape, bf16),
            pltpu.VMEM(payload.shape, f32),
            pltpu.SemaphoreType.DMA((3 + CHUNKS,)),
        ],
        compiler_params=params,
        cost_estimate=near_cost,
        name="direct",
    )(owner, column, line, blocks, every, every_other)
    others = lax.ppermute(direct, "col", swap)
    return pl.pallas_call(
        lambda *refs: finish_kernel(*refs, inner=inner),
        out_shape=shaped((sides, lanes), f32),
        in_specs=[VMEM] * 4,
        out_specs=VMEM,
        compiler_params=params,
        name="finish",
    )(parts, direct, others, basis_t)


def solution(mesh):
    parts, rows, cols = mesh.devices.shape
    x = 2 if rows % 2 == 0 else 1
    mesh = Mesh(mesh.devices.reshape(parts, rows // x, x, cols), ("parts", "z", "x", "col"))
    split = ("parts", "z", "x", "col")
    return jax.shard_map(
        shards,
        mesh=mesh,
        in_specs=(
            P(None, split),
            P(split, None, None),
            P(split, None, None),
            P(split, None),
            P(split, None),
            P(split, None),
            P(split, None),
            P(split, None),
            P(split, None),
        ),
        out_specs=P(None, split),
        check_vma=False,
    )
```

```python
import jax
import jax.numpy as jnp
from jax import lax
from jax.experimental import pallas as pl
from jax.experimental.pallas import tpu as pltpu
from jax.sharding import Mesh, PartitionSpec as P

f32 = jnp.float32
bf16 = jnp.bfloat16
LAST = (((1,), (1,)), ((), ()))
PLAIN = (((1,), (0,)), ((), ()))
FIRST = (((0,), (0,)), ((), ()))
HBM = pl.BlockSpec(memory_space=pltpu.HBM)
VMEM = pl.BlockSpec(memory_space=pltpu.VMEM)
EARLY, LATER = 1, 1
UNROLL = 48
GROUP = ("x", "col", "z")


def dot(left, right, dims):
    return lax.dot_general(left, right, dims, preferred_element_type=f32)


def halves(value):
    high = value.astype(bf16)
    return high, (value - high.astype(f32)).astype(bf16)


def one_hot(match):
    return match.astype(f32).astype(bf16)


def side_mask(sides, rank):
    row = lax.broadcasted_iota(jnp.int32, (sides, sides * rank), 0)
    lane = lax.broadcasted_iota(jnp.int32, (sides, sides * rank), 1)
    return lane // rank == row


def start(source, target, sem):
    copy = pltpu.make_async_copy(source, target, sem)
    copy.start()
    return copy


def in_hbm(array):
    return pltpu.with_memory_space_constraint(array, pltpu.HBM)


def slot_of(cluster, inner):
    depth, width = inner
    device = cluster >> 1
    return lax.rem(device, 2 * width) * depth + lax.div(device, 2 * width)


def each(count, body):
    if count <= 16:
        for d in range(count):
            body(d)
    else:
        pl.loop(0, count)(body)


def pack_kernel(
    cells_hbm, basis_hbm, first_hbm, second_hbm, coupling_hbm, blocks_hbm,
    out_hbm, mine_ref, far_ref, coupling_ref, early_ref,
    cells_ref, basis_ref, out_ref, sems, *, inner,
):
    copies = [
        start(cells_hbm, cells_ref, sems.at[0]),
        start(basis_hbm, basis_ref, sems.at[1]),
    ]
    ahead = [
        start(first_hbm, far_ref.at[0], sems.at[2]),
        start(second_hbm, far_ref.at[1], sems.at[3]),
        start(coupling_hbm, coupling_ref, sems.at[4]),
        start(blocks_hbm.at[pl.ds(0, early_ref.shape[0])], early_ref, sems.at[5]),
    ]
    sides = cells_ref.shape[0]
    owned, rank, width = basis_ref.shape
    mask = side_mask(sides, rank)
    for copy in copies:
        copy.wait()
    mine_ref[...] = cells_ref[...]
    blocks, lines = [], []
    for k in range(owned):
        cells = cells_ref[:, k * width : (k + 1) * width]
        blocks.append(cells.astype(f32))
        tiled = jnp.concatenate([basis_ref[k]] * sides, axis=0)
        every = dot(cells, tiled, LAST)
        flat = jnp.sum(jnp.where(mask, every, 0.0), axis=0, keepdims=True)
        lines += [flat[:, :128], flat[:, 128:]]
    moments = jnp.concatenate(lines, axis=0)
    high = moments.astype(bf16).astype(f32)
    moments = jnp.concatenate([high, moments - high], axis=0).astype(bf16)
    for c in range(2):
        half = jnp.concatenate([block[4 * c : 4 * c + 4] for block in blocks], axis=0).astype(bf16)
        for x in range(inner[1]):

            def store(z, c=c, x=x, half=half):
                d = (2 * x + c) * inner[0] + z
                out_ref[d, 0] = half
                out_ref[d, 1] = moments

            each(inner[0], store)
    start(out_ref, out_hbm, sems.at[0]).wait()
    for copy in ahead:
        copy.wait()


def start_indices(owner_hbm, col_hbm, row_hbm, owner, col, row, sems):
    return [
        start(owner_hbm, owner, sems.at[0]),
        start(col_hbm, col, sems.at[1]),
        start(row_hbm, row, sems.at[2]),
    ]


def near_copies(blocks_hbm, first, blocks_ref, chunks, sems):
    size = blocks_ref.shape[0] // chunks
    return [
        start(blocks_hbm.at[pl.ds(first + c * size, size)], blocks_ref.at[pl.ds(c * size, size)], sems.at[3 + c])
        for c in range(chunks)
    ]


def near_loop(first, size, body):
    unroll = min(UNROLL, size)

    def group(g, _):
        body([first + g * unroll + u for u in range(unroll)])
        return 0

    lax.fori_loop(0, size // unroll, group, 0)


def turn_kernel(
    far, coupling_ref, by_row_ref, by_col_ref, gather_ref, spread_ref, *, inner
):
    count, size = coupling_ref.shape
    rank = round(size**0.5)
    devices = gather_ref.shape[0] // 8
    source = lax.broadcasted_iota(jnp.int32, (8 * devices, count), 0)
    target = lax.broadcasted_iota(jnp.int32, (4 * devices, count), 0)
    for n in range(2):
        c = far[n]
        slot, k = slot_of(c, inner), c & 1
        for h in range(2):
            at = 8 * slot + 2 * k + h
            hot = one_hot((source == at) | (source == at + 4))
            gather_ref[:, (2 * n + h) * count : (2 * n + h + 1) * count] = hot
        at = 4 * slot + 2 * k
        hot = ((target == at) | (target == at + 1)).astype(f32).T.astype(bf16)
        spread_ref[2 * n * count : (2 * n + 1) * count, :] = hot
        spread_ref[(2 * n + 1) * count : (2 * n + 2) * count, :] = hot

    for t in range(0, size, 128):
        by_row_ref[t : t + 128, :] = coupling_ref[:, t : t + 128].astype(f32).T
    for k in range(rank):
        by_col_ref[k * rank : (k + 1) * rank, :] = by_row_ref[pl.ds(k, rank, stride=rank), :]


def mirror_kernel(
    owner_hbm, col_hbm, row_hbm, blocks_hbm, early_ref, mine_ref, other_ref,
    keep_ref, give_ref,
    owner, col, row, later_ref, cells_ref, sums_ref, sems, *, inner,
):
    early, width, _ = early_ref.shape
    chunk = early // EARLY
    indices = start_indices(owner_hbm, col_hbm, row_hbm, owner, col, row, sems)
    copies = near_copies(blocks_hbm, early, later_ref, LATER, sems)
    devices = keep_ref.shape[0]
    row_clusters = cells_ref.shape[0]
    me = lax.axis_index("col")
    for k in range(2):
        cells_ref[2 * me + k] = mine_ref[:, k * width : (k + 1) * width].astype(f32)
        cells_ref[2 - 2 * me + k] = other_ref[:, k * width : (k + 1) * width].astype(f32)
    sums_ref[...] = jnp.zeros(sums_ref.shape, f32)

    def multiply(source_ref, first):
        def body(group):
            done = []
            for p in group:
                j = owner[0, p] * row_clusters + col[0, p]
                at = 2 * slot_of(j, inner) + (j & 1)
                cells = cells_ref[row[0, p]].astype(bf16)
                done.append((at, dot(cells, source_ref[p - first], PLAIN)))
            for at, mirrored in done:
                sums_ref[at] += mirrored

        return body

    for copy in indices:
        copy.wait()
    near_loop(0, early, multiply(early_ref, 0))
    for c, copy in enumerate(copies):
        copy.wait()
        near_loop(early + c * chunk, chunk, multiply(later_ref, early))

    def store(d):
        for k in range(2):
            keep_ref[d, k] = sums_ref[2 * d + k, pl.ds(4 * me, 4), :]
            give_ref[d, k] = sums_ref[2 * d + k, pl.ds(4 - 4 * me, 4), :]

    each(devices, store)


def far_kernel(
    every_ref, gather_ref, spread_ref, by_row_ref, by_col_ref, keep_ref, got_ref,
    out_hbm, near_ref, left_ref, right_ref, lines_ref, far_ref, sems,
):
    near_ref[...] = keep_ref[...] + got_ref[...]
    near = start(near_ref, out_hbm.at[:, pl.ds(0, 2)], sems.at[0])
    devices = every_ref.shape[0]
    size, count = left_ref.shape
    sides = 8
    rank = size // sides

    lines = every_ref[:, 1].astype(f32).reshape(8 * devices, 128).astype(bf16)
    moments = dot(lines, gather_ref[...], FIRST)
    for h in range(2):
        left_ref[h * 128 : (h + 1) * 128, :] = moments[:, h * count : (h + 1) * count]
        right_ref[h * 128 : (h + 1) * 128, :] = moments[:, (2 + h) * count : (3 + h) * count]

    lines = []
    for h in range(2):
        total = 0.0
        for n, (matrix_ref, source_ref) in enumerate(((by_col_ref, right_ref), (by_row_ref, left_ref))):
            sums = [jnp.zeros((rank, count), f32) for _ in range(sides // 2)]
            for r in range(rank):
                matrix = matrix_ref[r * rank : (r + 1) * rank, :]
                for s in range(sides // 2):
                    at = h * 128 + s * rank + r
                    sums[s] = sums[s] + source_ref[at : at + 1, :] * matrix
            pair = jnp.concatenate(halves(jnp.concatenate(sums, axis=0)), axis=1)
            total = total + dot(pair, spread_ref[2 * n * count : (2 * n + 2) * count, :], PLAIN)
        lines.append(total)
    odd = lax.broadcasted_iota(jnp.int32, (128, 4 * devices), 1) % 2 == 1
    lines_ref[...] = jnp.where(odd, lines[1], lines[0]).T

    def store(d):
        far_ref[d, 0] = lines_ref[pl.ds(4 * d, 4), :]

    each(devices, store)
    far = start(far_ref, out_hbm.at[:, pl.ds(2, 1)], sems.at[1])
    near.wait()
    far.wait()


def direct_kernel(
    owner_hbm, col_hbm, row_hbm, blocks_hbm, every_ref, others_ref,
    out_ref, owner, col, row, blocks_ref, cells_ref, sems, *, inner,
):
    indices = start_indices(owner_hbm, col_hbm, row_hbm, owner, col, row, sems)
    copies = near_copies(blocks_hbm, 0, blocks_ref, EARLY + LATER, sems)
    chunk = blocks_ref.shape[0] // (EARLY + LATER)
    row_clusters = out_ref.shape[0]
    out_ref[...] = jnp.zeros(out_ref.shape, f32)
    me = lax.axis_index("col")

    def load(d):
        mine, other = every_ref[d, 0].astype(f32), others_ref[d, 0].astype(f32)
        first, second = jnp.where(me == 0, mine, other), jnp.where(me == 0, other, mine)
        for k in range(2):
            cells_ref[d, k] = jnp.concatenate([first[4 * k : 4 * k + 4], second[4 * k : 4 * k + 4]], axis=0)

    each(every_ref.shape[0], load)
    for copy in indices:
        copy.wait()

    def body(group):
        done = []
        for p in group:
            j = owner[0, p] * row_clusters + col[0, p]
            cells = cells_ref[slot_of(j, inner), j & 1].astype(bf16)
            done.append((row[0, p], dot(cells, blocks_ref[p], LAST)))
        for i, direct in done:
            out_ref[i] += direct

    for c, copy in enumerate(copies):
        copy.wait()
        near_loop(c * chunk, chunk, body)


def finish_kernel(parts_ref, mine_ref, other_ref, basis_ref, out_ref, *, inner):
    owned, rank, width = basis_ref.shape
    sides = out_ref.shape[0]
    depth = inner[0]
    near, far = [], jnp.zeros((4, 128), f32)
    for c in range(2):
        totals = (jnp.zeros((4, 128), f32), jnp.zeros((4, 128), f32), far)
        for x in range(inner[1]):

            def add(z, totals, first=(2 * x + c) * depth):
                return tuple(total + parts_ref[first + z, b] for b, total in enumerate(totals))

            totals = lax.fori_loop(0, depth, add, totals, unroll=min(8, depth))
        near.append(totals[:2])
        far = totals[2]
    me = lax.axis_index("col")
    mask = side_mask(sides, rank)
    for k in range(owned):
        total = jnp.concatenate([near[0][k], near[1][k]], axis=0)
        total = total + (mine_ref[2 * me + k] + other_ref[2 * me + k])
        flat = jnp.concatenate([far[2 * k : 2 * k + 1], far[2 * k + 1 : 2 * k + 2]], axis=1)
        high, low = halves(jnp.where(mask, flat, 0.0))
        tiled = jnp.concatenate([basis_ref[k]] * sides, axis=0)
        total = total + (dot(high, tiled, PLAIN) + dot(low, tiled, PLAIN))
        out_ref[:, k * width : (k + 1) * width] = total


def shards(cells, basis_t, near_blocks, near_owner, near_col, near_row, far_row, far_col, coupling):
    depth = lax.axis_size("z")
    inner = (depth, lax.axis_size("x"))
    devices = 2 * depth * inner[1]
    sides, lanes = cells.shape
    owned, rank, width = basis_t.shape
    row_clusters = owned * lax.axis_size("col")
    pairs = near_blocks.shape[0]
    count = coupling.shape[0]
    swap = [(0, 1), (1, 0)]
    params = pltpu.CompilerParams(vmem_limit_bytes=24 * 1024 * 1024)

    def shaped(shape, dtype):
        return jax.ShapeDtypeStruct(shape, dtype)

    def exchange(blocks):
        return lax.all_to_all(blocks, GROUP, split_axis=0, concat_axis=0, tiled=True)

    turn_cost = pl.CostEstimate(flops=10**6, bytes_accessed=3 * 10**6, transcendentals=0)
    near_cost = pl.CostEstimate(
        flops=2 * pairs * sides * width * width, bytes_accessed=10**7, transcendentals=0
    )
    payload = shaped((devices, 2, sides, 128), bf16)
    owner, column, line = [in_hbm(a.reshape(1, pairs)) for a in (near_owner, near_col, near_row)]
    first, second = [in_hbm(a.reshape(1, count)) for a in (far_row, far_col)]
    blocks = in_hbm(near_blocks)
    part = pairs // (EARLY + LATER)
    block = near_blocks.shape[1:]
    index_scratch = [pltpu.SMEM((1, pairs), jnp.int32)] * 3
    packed, mine, far, couplings, early_blocks = pl.pallas_call(
        lambda *refs: pack_kernel(*refs, inner=inner),
        out_shape=[
            payload,
            shaped(cells.shape, bf16),
            shaped((2, 1, count), jnp.int32),
            shaped(coupling.shape, bf16),
            shaped((EARLY * part,) + block, bf16),
        ],
        in_specs=[HBM] * 6,
        out_specs=[HBM] + [VMEM] * 4,
        scratch_shapes=[
            pltpu.VMEM(cells.shape, bf16),
            pltpu.VMEM(basis_t.shape, bf16),
            pltpu.VMEM(payload.shape, bf16),
            pltpu.SemaphoreType.DMA((6,)),
        ],
        compiler_params=params,
        name="pack",
    )(in_hbm(cells), in_hbm(basis_t), first, second, in_hbm(coupling), blocks)
    every = exchange(packed)
    other = lax.ppermute(mine, "col", swap)
    by_row, by_col, gather, spread = pl.pallas_call(
        lambda *refs: turn_kernel(*refs, inner=inner),
        out_shape=[
            shaped((rank * rank, count), f32),
            shaped((rank * rank, count), f32),
            shaped((8 * devices, 4 * count), bf16),
            shaped((4 * count, 4 * devices), bf16),
        ],
        in_specs=[VMEM] * 2,
        out_specs=[VMEM] * 4,
        compiler_params=params,
        cost_estimate=turn_cost,
        name="turn",
    )(far, couplings)
    keep, give = pl.pallas_call(
        lambda *refs: mirror_kernel(*refs, inner=inner),
        out_shape=[shaped((devices, 2, 4, 128), f32)] * 2,
        in_specs=[HBM] * 4 + [VMEM] * 3,
        out_specs=[VMEM] * 2,
        scratch_shapes=index_scratch
        + [
            pltpu.VMEM((LATER * part,) + block, bf16),
            pltpu.VMEM((row_clusters, sides, width), f32),
            pltpu.VMEM((2 * devices, sides, width), f32),
            pltpu.SemaphoreType.DMA((3 + LATER,)),
        ],
        compiler_params=params,
        cost_estimate=near_cost,
        name="mirror",
    )(owner, column, line, blocks, early_blocks, mine, other)
    got = lax.ppermute(give, "col", swap)
    partial = pl.pallas_call(
        far_kernel,
        out_shape=shaped((devices, 3, 4, 128), f32),
        in_specs=[VMEM] * 7,
        out_specs=HBM,
        scratch_shapes=[pltpu.VMEM(keep.shape, f32)]
        + [pltpu.VMEM((sides * rank, count), f32)] * 2
        + [
            pltpu.VMEM((4 * devices, 128), f32),
            pltpu.VMEM((devices, 1, 4, 128), f32),
            pltpu.SemaphoreType.DMA((2,)),
        ],
        compiler_params=params,
        name="far",
    )(every, gather, spread, by_row, by_col, keep, got)
    parts = exchange(partial)
    every_other = lax.ppermute(every, "col", swap)
    direct = pl.pallas_call(
        lambda *refs: direct_kernel(*refs, inner=inner),
        out_shape=shaped((row_clusters, sides, width), f32),
        in_specs=[HBM] * 4 + [VMEM] * 2,
        out_specs=VMEM,
        scratch_shapes=index_scratch
        + [
            pltpu.VMEM(near_blocks.shape, bf16),
            pltpu.VMEM(payload.shape, f32),
            pltpu.SemaphoreType.DMA((3 + EARLY + LATER,)),
        ],
        compiler_params=params,
        cost_estimate=near_cost,
        name="direct",
    )(owner, column, line, blocks, every, every_other)
    others = lax.ppermute(direct, "col", swap)
    return pl.pallas_call(
        lambda *refs: finish_kernel(*refs, inner=inner),
        out_shape=shaped((sides, lanes), f32),
        in_specs=[VMEM] * 4,
        out_specs=VMEM,
        compiler_params=params,
        name="finish",
    )(parts, direct, others, basis_t)


def solution(mesh):
    parts, rows, cols = mesh.devices.shape
    x = 2 if rows % 2 == 0 else 1
    mesh = Mesh(mesh.devices.reshape(parts, rows // x, x, cols), ("parts", "z", "x", "col"))
    split = ("parts", "z", "x", "col")
    return jax.shard_map(
        shards,
        mesh=mesh,
        in_specs=(
            P(None, split),
            P(split, None, None),
            P(split, None, None),
            P(split, None),
            P(split, None),
            P(split, None),
            P(split, None),
            P(split, None),
            P(split, None),
        ),
        out_specs=P(None, split),
        check_vma=False,
    )
```

```python
import jax
import jax.numpy as jnp
from jax import lax
from jax.experimental import pallas as pl
from jax.experimental.pallas import tpu as pltpu
from jax.sharding import Mesh, PartitionSpec as P

f32 = jnp.float32
bf16 = jnp.bfloat16
LAST = (((1,), (1,)), ((), ()))
PLAIN = (((1,), (0,)), ((), ()))
FIRST = (((0,), (0,)), ((), ()))
HBM = pl.BlockSpec(memory_space=pltpu.HBM)
VMEM = pl.BlockSpec(memory_space=pltpu.VMEM)
EARLY, LATER = 1, 1
UNROLL = 48
GROUP = ("x", "col", "z")


def dot(left, right, dims):
    return lax.dot_general(left, right, dims, preferred_element_type=f32)


def halves(value):
    high = value.astype(bf16)
    return high, (value - high.astype(f32)).astype(bf16)


def one_hot(match):
    return match.astype(f32).astype(bf16)


def side_mask(sides, rank):
    row = lax.broadcasted_iota(jnp.int32, (sides, sides * rank), 0)
    lane = lax.broadcasted_iota(jnp.int32, (sides, sides * rank), 1)
    return lane // rank == row


def start(source, target, sem):
    copy = pltpu.make_async_copy(source, target, sem)
    copy.start()
    return copy


def in_hbm(array):
    return pltpu.with_memory_space_constraint(array, pltpu.HBM)


def slot_of(cluster, inner):
    depth, width = inner
    device = cluster >> 1
    return lax.rem(device, 2 * width) * depth + lax.div(device, 2 * width)


def each(count, body):
    if count <= 16:
        for d in range(count):
            body(d)
    else:
        pl.loop(0, count)(body)


def pack_kernel(
    cells_hbm, basis_hbm, first_hbm, second_hbm, coupling_hbm, blocks_hbm,
    out_hbm, mine_ref, far_ref, coupling_ref, early_ref,
    cells_ref, basis_ref, out_ref, sems, *, inner,
):
    copies = [
        start(cells_hbm, cells_ref, sems.at[0]),
        start(basis_hbm, basis_ref, sems.at[1]),
    ]
    ahead = [
        start(first_hbm, far_ref.at[0], sems.at[2]),
        start(second_hbm, far_ref.at[1], sems.at[3]),
        start(coupling_hbm, coupling_ref, sems.at[4]),
        start(blocks_hbm.at[pl.ds(0, early_ref.shape[0])], early_ref, sems.at[5]),
    ]
    sides = cells_ref.shape[0]
    owned, rank, width = basis_ref.shape
    mask = side_mask(sides, rank)
    for copy in copies:
        copy.wait()
    mine_ref[...] = cells_ref[...]
    blocks, lines = [], []
    for k in range(owned):
        cells = cells_ref[:, k * width : (k + 1) * width]
        blocks.append(cells.astype(f32))
        tiled = jnp.concatenate([basis_ref[k]] * sides, axis=0)
        every = dot(cells, tiled, LAST)
        flat = jnp.sum(jnp.where(mask, every, 0.0), axis=0, keepdims=True)
        lines += [flat[:, :128], flat[:, 128:]]
    moments = jnp.concatenate(lines, axis=0)
    high = moments.astype(bf16).astype(f32)
    moments = jnp.concatenate([high, moments - high], axis=0).astype(bf16)
    for c in range(2):
        half = jnp.concatenate([block[4 * c : 4 * c + 4] for block in blocks], axis=0).astype(bf16)
        for x in range(inner[1]):

            def store(z, c=c, x=x, half=half):
                d = (2 * x + c) * inner[0] + z
                out_ref[d, 0] = half
                out_ref[d, 1] = moments

            each(inner[0], store)
    start(out_ref, out_hbm, sems.at[0]).wait()
    for copy in ahead:
        copy.wait()


def start_indices(owner_hbm, col_hbm, row_hbm, owner, col, row, sems):
    return [
        start(owner_hbm, owner, sems.at[0]),
        start(col_hbm, col, sems.at[1]),
        start(row_hbm, row, sems.at[2]),
    ]


def near_copies(blocks_hbm, first, blocks_ref, chunks, sems):
    size = blocks_ref.shape[0] // chunks
    return [
        start(blocks_hbm.at[pl.ds(first + c * size, size)], blocks_ref.at[pl.ds(c * size, size)], sems.at[3 + c])
        for c in range(chunks)
    ]


def near_loop(first, size, body):
    unroll = min(UNROLL, size)

    def group(g, _):
        body([first + g * unroll + u for u in range(unroll)])
        return 0

    lax.fori_loop(0, size // unroll, group, 0)


def turn_kernel(
    far, coupling_ref, by_row_ref, by_col_ref, gather_ref, spread_ref, *, inner
):
    count, size = coupling_ref.shape
    rank = round(size**0.5)
    devices = gather_ref.shape[0] // 8
    source = lax.broadcasted_iota(jnp.int32, (8 * devices, count), 0)
    target = lax.broadcasted_iota(jnp.int32, (4 * devices, count), 0)
    for n in range(2):
        c = far[n]
        slot, k = slot_of(c, inner), c & 1
        for h in range(2):
            at = 8 * slot + 2 * k + h
            hot = one_hot((source == at) | (source == at + 4))
            gather_ref[:, (2 * n + h) * count : (2 * n + h + 1) * count] = hot
        at = 4 * slot + 2 * k
        hot = ((target == at) | (target == at + 1)).astype(f32).T.astype(bf16)
        spread_ref[2 * n * count : (2 * n + 1) * count, :] = hot
        spread_ref[(2 * n + 1) * count : (2 * n + 2) * count, :] = hot

    for t in range(0, size, 128):
        by_row_ref[t : t + 128, :] = coupling_ref[:, t : t + 128].astype(f32).T
    for k in range(rank):
        by_col_ref[k * rank : (k + 1) * rank, :] = by_row_ref[pl.ds(k, rank, stride=rank), :]


def mirror_kernel(
    owner_hbm, col_hbm, row_hbm, blocks_hbm, early_ref, mine_ref, other_ref,
    keep_ref, give_ref,
    owner, col, row, later_ref, cells_ref, sums_ref, sems, *, inner,
):
    early, width, _ = early_ref.shape
    chunk = early // EARLY
    indices = start_indices(owner_hbm, col_hbm, row_hbm, owner, col, row, sems)
    copies = near_copies(blocks_hbm, early, later_ref, LATER, sems)
    devices = keep_ref.shape[0]
    row_clusters = cells_ref.shape[0]
    me = lax.axis_index("col")
    for k in range(2):
        cells_ref[2 * me + k] = mine_ref[:, k * width : (k + 1) * width].astype(f32)
        cells_ref[2 - 2 * me + k] = other_ref[:, k * width : (k + 1) * width].astype(f32)
    sums_ref[...] = jnp.zeros(sums_ref.shape, f32)

    def multiply(source_ref, first):
        def body(group):
            done = []
            for p in group:
                j = owner[0, p] * row_clusters + col[0, p]
                at = 2 * slot_of(j, inner) + (j & 1)
                cells = cells_ref[row[0, p]].astype(bf16)
                done.append((at, dot(cells, source_ref[p - first], PLAIN)))
            for at, mirrored in done:
                sums_ref[at] += mirrored

        return body

    for copy in indices:
        copy.wait()
    near_loop(0, early, multiply(early_ref, 0))
    for c, copy in enumerate(copies):
        copy.wait()
        near_loop(early + c * chunk, chunk, multiply(later_ref, early))

    def store(d):
        for k in range(2):
            keep_ref[d, k] = sums_ref[2 * d + k, pl.ds(4 * me, 4), :]
            give_ref[d, k] = sums_ref[2 * d + k, pl.ds(4 - 4 * me, 4), :]

    each(devices, store)


def far_kernel(
    every_ref, gather_ref, spread_ref, by_row_ref, by_col_ref,
    far_ref, left_ref, right_ref, lines_ref,
):
    devices = every_ref.shape[0]
    size, count = left_ref.shape
    sides = 8
    rank = size // sides

    lines = every_ref[:, 1].astype(f32).reshape(8 * devices, 128).astype(bf16)
    moments = dot(lines, gather_ref[...], FIRST)
    for h in range(2):
        left_ref[h * 128 : (h + 1) * 128, :] = moments[:, h * count : (h + 1) * count]
        right_ref[h * 128 : (h + 1) * 128, :] = moments[:, (2 + h) * count : (3 + h) * count]

    lines = []
    for h in range(2):
        total = 0.0
        for n, (matrix_ref, source_ref) in enumerate(((by_col_ref, right_ref), (by_row_ref, left_ref))):
            sums = [jnp.zeros((rank, count), f32) for _ in range(sides // 2)]
            for r in range(rank):
                matrix = matrix_ref[r * rank : (r + 1) * rank, :]
                for s in range(sides // 2):
                    at = h * 128 + s * rank + r
                    sums[s] = sums[s] + source_ref[at : at + 1, :] * matrix
            pair = jnp.concatenate(halves(jnp.concatenate(sums, axis=0)), axis=1)
            total = total + dot(pair, spread_ref[2 * n * count : (2 * n + 2) * count, :], PLAIN)
        lines.append(total)
    odd = lax.broadcasted_iota(jnp.int32, (128, 4 * devices), 1) % 2 == 1
    lines_ref[...] = jnp.where(odd, lines[1], lines[0]).T

    def store(d):
        far_ref[d, 0] = lines_ref[pl.ds(4 * d, 4), :]

    each(devices, store)

def join_kernel(far_ref, keep_ref, got_ref, out_hbm, near_ref, sems):
    far = start(far_ref, out_hbm.at[:, pl.ds(2, 1)], sems.at[0])
    near_ref[...] = keep_ref[...] + got_ref[...]
    near = start(near_ref, out_hbm.at[:, pl.ds(0, 2)], sems.at[1])
    far.wait()
    near.wait()


def direct_kernel(
    owner_hbm, col_hbm, row_hbm, blocks_hbm, every_ref, others_ref,
    out_ref, owner, col, row, blocks_ref, cells_ref, sems, *, inner,
):
    indices = start_indices(owner_hbm, col_hbm, row_hbm, owner, col, row, sems)
    copies = near_copies(blocks_hbm, 0, blocks_ref, EARLY + LATER, sems)
    chunk = blocks_ref.shape[0] // (EARLY + LATER)
    row_clusters = out_ref.shape[0]
    out_ref[...] = jnp.zeros(out_ref.shape, f32)
    me = lax.axis_index("col")

    def load(d):
        mine, other = every_ref[d, 0].astype(f32), others_ref[d, 0].astype(f32)
        first, second = jnp.where(me == 0, mine, other), jnp.where(me == 0, other, mine)
        for k in range(2):
            cells_ref[d, k] = jnp.concatenate([first[4 * k : 4 * k + 4], second[4 * k : 4 * k + 4]], axis=0)

    each(every_ref.shape[0], load)
    for copy in indices:
        copy.wait()

    def body(group):
        done = []
        for p in group:
            j = owner[0, p] * row_clusters + col[0, p]
            cells = cells_ref[slot_of(j, inner), j & 1].astype(bf16)
            done.append((row[0, p], dot(cells, blocks_ref[p], LAST)))
        for i, direct in done:
            out_ref[i] += direct

    for c, copy in enumerate(copies):
        copy.wait()
        near_loop(c * chunk, chunk, body)


def finish_kernel(parts_ref, mine_ref, other_ref, basis_ref, out_ref, *, inner):
    owned, rank, width = basis_ref.shape
    sides = out_ref.shape[0]
    depth = inner[0]
    near, far = [], jnp.zeros((4, 128), f32)
    for c in range(2):
        totals = (jnp.zeros((4, 128), f32), jnp.zeros((4, 128), f32), far)
        for x in range(inner[1]):

            def add(z, totals, first=(2 * x + c) * depth):
                return tuple(total + parts_ref[first + z, b] for b, total in enumerate(totals))

            totals = lax.fori_loop(0, depth, add, totals, unroll=min(8, depth))
        near.append(totals[:2])
        far = totals[2]
    me = lax.axis_index("col")
    mask = side_mask(sides, rank)
    for k in range(owned):
        total = jnp.concatenate([near[0][k], near[1][k]], axis=0)
        total = total + (mine_ref[2 * me + k] + other_ref[2 * me + k])
        flat = jnp.concatenate([far[2 * k : 2 * k + 1], far[2 * k + 1 : 2 * k + 2]], axis=1)
        high, low = halves(jnp.where(mask, flat, 0.0))
        tiled = jnp.concatenate([basis_ref[k]] * sides, axis=0)
        total = total + (dot(high, tiled, PLAIN) + dot(low, tiled, PLAIN))
        out_ref[:, k * width : (k + 1) * width] = total


def shards(cells, basis_t, near_blocks, near_owner, near_col, near_row, far_row, far_col, coupling):
    depth = lax.axis_size("z")
    inner = (depth, lax.axis_size("x"))
    devices = 2 * depth * inner[1]
    sides, lanes = cells.shape
    owned, rank, width = basis_t.shape
    row_clusters = owned * lax.axis_size("col")
    pairs = near_blocks.shape[0]
    count = coupling.shape[0]
    swap = [(0, 1), (1, 0)]
    params = pltpu.CompilerParams(vmem_limit_bytes=24 * 1024 * 1024)

    def shaped(shape, dtype):
        return jax.ShapeDtypeStruct(shape, dtype)

    def exchange(blocks):
        return lax.all_to_all(blocks, GROUP, split_axis=0, concat_axis=0, tiled=True)

    turn_cost = pl.CostEstimate(flops=10**6, bytes_accessed=3 * 10**6, transcendentals=0)
    near_cost = pl.CostEstimate(
        flops=2 * pairs * sides * width * width, bytes_accessed=10**7, transcendentals=0
    )
    payload = shaped((devices, 2, sides, 128), bf16)
    owner, column, line = [in_hbm(a.reshape(1, pairs)) for a in (near_owner, near_col, near_row)]
    first, second = [in_hbm(a.reshape(1, count)) for a in (far_row, far_col)]
    blocks = in_hbm(near_blocks)
    part = pairs // (EARLY + LATER)
    block = near_blocks.shape[1:]
    index_scratch = [pltpu.SMEM((1, pairs), jnp.int32)] * 3
    packed, mine, far, couplings, early_blocks = pl.pallas_call(
        lambda *refs: pack_kernel(*refs, inner=inner),
        out_shape=[
            payload,
            shaped(cells.shape, bf16),
            shaped((2, 1, count), jnp.int32),
            shaped(coupling.shape, bf16),
            shaped((EARLY * part,) + block, bf16),
        ],
        in_specs=[HBM] * 6,
        out_specs=[HBM] + [VMEM] * 4,
        scratch_shapes=[
            pltpu.VMEM(cells.shape, bf16),
            pltpu.VMEM(basis_t.shape, bf16),
            pltpu.VMEM(payload.shape, bf16),
            pltpu.SemaphoreType.DMA((6,)),
        ],
        compiler_params=params,
        name="pack",
    )(in_hbm(cells), in_hbm(basis_t), first, second, in_hbm(coupling), blocks)
    every = exchange(packed)
    other = lax.ppermute(mine, "col", swap)
    by_row, by_col, gather, spread = pl.pallas_call(
        lambda *refs: turn_kernel(*refs, inner=inner),
        out_shape=[
            shaped((rank * rank, count), f32),
            shaped((rank * rank, count), f32),
            shaped((8 * devices, 4 * count), bf16),
            shaped((4 * count, 4 * devices), bf16),
        ],
        in_specs=[VMEM] * 2,
        out_specs=[VMEM] * 4,
        compiler_params=params,
        cost_estimate=turn_cost,
        name="turn",
    )(far, couplings)
    keep, give = pl.pallas_call(
        lambda *refs: mirror_kernel(*refs, inner=inner),
        out_shape=[shaped((devices, 2, 4, 128), f32)] * 2,
        in_specs=[HBM] * 4 + [VMEM] * 3,
        out_specs=[VMEM] * 2,
        scratch_shapes=index_scratch
        + [
            pltpu.VMEM((LATER * part,) + block, bf16),
            pltpu.VMEM((row_clusters, sides, width), f32),
            pltpu.VMEM((2 * devices, sides, width), f32),
            pltpu.SemaphoreType.DMA((3 + LATER,)),
        ],
        compiler_params=params,
        cost_estimate=near_cost,
        name="mirror",
    )(owner, column, line, blocks, early_blocks, mine, other)
    got = lax.ppermute(give, "col", swap)
    coupled = pl.pallas_call(
        far_kernel,
        out_shape=shaped((devices, 1, 4, 128), f32),
        in_specs=[VMEM] * 5,
        out_specs=VMEM,
        scratch_shapes=[pltpu.VMEM((sides * rank, count), f32)] * 2 + [pltpu.VMEM((4 * devices, 128), f32)],
        compiler_params=params,
        cost_estimate=turn_cost,
        name="far",
    )(every, gather, spread, by_row, by_col)
    partial = pl.pallas_call(
        join_kernel,
        out_shape=shaped((devices, 3, 4, 128), f32),
        in_specs=[VMEM] * 3,
        out_specs=HBM,
        scratch_shapes=[pltpu.VMEM(keep.shape, f32), pltpu.SemaphoreType.DMA((2,))],
        compiler_params=params,
        name="join",
    )(coupled, keep, got)
    parts = exchange(partial)
    every_other = lax.ppermute(every, "col", swap)
    direct = pl.pallas_call(
        lambda *refs: direct_kernel(*refs, inner=inner),
        out_shape=shaped((row_clusters, sides, width), f32),
        in_specs=[HBM] * 4 + [VMEM] * 2,
        out_specs=VMEM,
        scratch_shapes=index_scratch
        + [
            pltpu.VMEM(near_blocks.shape, bf16),
            pltpu.VMEM(payload.shape, f32),
            pltpu.SemaphoreType.DMA((3 + EARLY + LATER,)),
        ],
        compiler_params=params,
        cost_estimate=near_cost,
        name="direct",
    )(owner, column, line, blocks, every, every_other)
    others = lax.ppermute(direct, "col", swap)
    return pl.pallas_call(
        lambda *refs: finish_kernel(*refs, inner=inner),
        out_shape=shaped((sides, lanes), f32),
        in_specs=[VMEM] * 4,
        out_specs=VMEM,
        compiler_params=params,
        name="finish",
    )(parts, direct, others, basis_t)


def solution(mesh):
    parts, rows, cols = mesh.devices.shape
    x = 2 if rows % 2 == 0 else 1
    mesh = Mesh(mesh.devices.reshape(parts, rows // x, x, cols), ("parts", "z", "x", "col"))
    split = ("parts", "z", "x", "col")
    return jax.shard_map(
        shards,
        mesh=mesh,
        in_specs=(
            P(None, split),
            P(split, None, None),
            P(split, None, None),
            P(split, None),
            P(split, None),
            P(split, None),
            P(split, None),
            P(split, None),
            P(split, None),
        ),
        out_specs=P(None, split),
        check_vma=False,
    )
```

```python
import jax
import jax.numpy as jnp
from jax import lax
from jax.experimental import pallas as pl
from jax.experimental.pallas import tpu as pltpu
from jax.sharding import Mesh, PartitionSpec as P

f32 = jnp.float32
bf16 = jnp.bfloat16
LAST = (((1,), (1,)), ((), ()))
PLAIN = (((1,), (0,)), ((), ()))
FIRST = (((0,), (0,)), ((), ()))
HBM = pl.BlockSpec(memory_space=pltpu.HBM)
VMEM = pl.BlockSpec(memory_space=pltpu.VMEM)
EARLY, LATER = 1, 1
UNROLL = 48
GROUP = ("x", "col", "z")


def dot(left, right, dims):
    return lax.dot_general(left, right, dims, preferred_element_type=f32)


def halves(value):
    high = value.astype(bf16)
    return high, (value - high.astype(f32)).astype(bf16)


def one_hot(match):
    return match.astype(f32).astype(bf16)


def side_mask(sides, rank):
    row = lax.broadcasted_iota(jnp.int32, (sides, sides * rank), 0)
    lane = lax.broadcasted_iota(jnp.int32, (sides, sides * rank), 1)
    return lane // rank == row


def start(source, target, sem):
    copy = pltpu.make_async_copy(source, target, sem)
    copy.start()
    return copy


def in_hbm(array):
    return pltpu.with_memory_space_constraint(array, pltpu.HBM)


def slot_of(cluster, inner):
    depth, width = inner
    device = cluster >> 1
    return lax.rem(device, 2 * width) * depth + lax.div(device, 2 * width)


def each(count, body):
    if count <= 16:
        for d in range(count):
            body(d)
    else:
        pl.loop(0, count)(body)


def pack_kernel(
    cells_hbm, basis_hbm, first_hbm, second_hbm, blocks_hbm,
    out_hbm, mine_ref, far_ref, early_ref,
    cells_ref, basis_ref, out_ref, sems, *, inner,
):
    copies = [
        start(cells_hbm, cells_ref, sems.at[0]),
        start(basis_hbm, basis_ref, sems.at[1]),
    ]
    ahead = [
        start(first_hbm, far_ref.at[0], sems.at[2]),
        start(second_hbm, far_ref.at[1], sems.at[3]),
        start(blocks_hbm.at[pl.ds(0, early_ref.shape[0])], early_ref, sems.at[5]),
    ]
    sides = cells_ref.shape[0]
    owned, rank, width = basis_ref.shape
    mask = side_mask(sides, rank)
    for copy in copies:
        copy.wait()
    mine_ref[...] = cells_ref[...]
    blocks, lines = [], []
    for k in range(owned):
        cells = cells_ref[:, k * width : (k + 1) * width]
        blocks.append(cells.astype(f32))
        tiled = jnp.concatenate([basis_ref[k]] * sides, axis=0)
        every = dot(cells, tiled, LAST)
        flat = jnp.sum(jnp.where(mask, every, 0.0), axis=0, keepdims=True)
        lines += [flat[:, :128], flat[:, 128:]]
    moments = jnp.concatenate(lines, axis=0)
    high = moments.astype(bf16).astype(f32)
    moments = jnp.concatenate([high, moments - high], axis=0).astype(bf16)
    for c in range(2):
        half = jnp.concatenate([block[4 * c : 4 * c + 4] for block in blocks], axis=0).astype(bf16)
        for x in range(inner[1]):

            def store(z, c=c, x=x, half=half):
                d = (2 * x + c) * inner[0] + z
                out_ref[d, 0] = half
                out_ref[d, 1] = moments

            each(inner[0], store)
    start(out_ref, out_hbm, sems.at[0]).wait()
    for copy in ahead:
        copy.wait()


def start_indices(owner_hbm, col_hbm, row_hbm, owner, col, row, sems):
    return [
        start(owner_hbm, owner, sems.at[0]),
        start(col_hbm, col, sems.at[1]),
        start(row_hbm, row, sems.at[2]),
    ]


def near_copies(blocks_hbm, first, blocks_ref, chunks, sems):
    size = blocks_ref.shape[0] // chunks
    return [
        start(blocks_hbm.at[pl.ds(first + c * size, size)], blocks_ref.at[pl.ds(c * size, size)], sems.at[3 + c])
        for c in range(chunks)
    ]


def near_loop(first, size, body):
    unroll = min(UNROLL, size)

    def group(g, _):
        body([first + g * unroll + u for u in range(unroll)])
        return 0

    lax.fori_loop(0, size // unroll, group, 0)


def turn_kernel(
    far, coupling_hbm, by_row_ref, by_col_ref, gather_ref, spread_ref, coupling_ref, sem, *, inner
):
    copy = start(coupling_hbm, coupling_ref, sem)
    count, size = coupling_ref.shape
    rank = round(size**0.5)
    devices = gather_ref.shape[0] // 8
    source = lax.broadcasted_iota(jnp.int32, (8 * devices, count), 0)
    target = lax.broadcasted_iota(jnp.int32, (4 * devices, count), 0)
    for n in range(2):
        c = far[n]
        slot, k = slot_of(c, inner), c & 1
        for h in range(2):
            at = 8 * slot + 2 * k + h
            hot = one_hot((source == at) | (source == at + 4))
            gather_ref[:, (2 * n + h) * count : (2 * n + h + 1) * count] = hot
        at = 4 * slot + 2 * k
        hot = ((target == at) | (target == at + 1)).astype(f32).T.astype(bf16)
        spread_ref[2 * n * count : (2 * n + 1) * count, :] = hot
        spread_ref[(2 * n + 1) * count : (2 * n + 2) * count, :] = hot

    copy.wait()
    for t in range(0, size, 128):
        by_row_ref[t : t + 128, :] = coupling_ref[:, t : t + 128].astype(f32).T
    for k in range(rank):
        by_col_ref[k * rank : (k + 1) * rank, :] = by_row_ref[pl.ds(k, rank, stride=rank), :]


def mirror_kernel(
    owner_hbm, col_hbm, row_hbm, blocks_hbm, early_ref, mine_ref, other_ref, _,
    keep_ref, give_ref,
    owner, col, row, later_ref, cells_ref, sums_ref, sems, *, inner,
):
    early, width, _ = early_ref.shape
    chunk = early // EARLY
    indices = start_indices(owner_hbm, col_hbm, row_hbm, owner, col, row, sems)
    copies = near_copies(blocks_hbm, early, later_ref, LATER, sems)
    devices = keep_ref.shape[0]
    row_clusters = cells_ref.shape[0]
    me = lax.axis_index("col")
    for k in range(2):
        cells_ref[2 * me + k] = mine_ref[:, k * width : (k + 1) * width].astype(f32)
        cells_ref[2 - 2 * me + k] = other_ref[:, k * width : (k + 1) * width].astype(f32)
    sums_ref[...] = jnp.zeros(sums_ref.shape, f32)

    def multiply(source_ref, first):
        def body(group):
            done = []
            for p in group:
                j = owner[0, p] * row_clusters + col[0, p]
                at = 2 * slot_of(j, inner) + (j & 1)
                cells = cells_ref[row[0, p]].astype(bf16)
                done.append((at, dot(cells, source_ref[p - first], PLAIN)))
            for at, mirrored in done:
                sums_ref[at] += mirrored

        return body

    for copy in indices:
        copy.wait()
    near_loop(0, early, multiply(early_ref, 0))
    for c, copy in enumerate(copies):
        copy.wait()
        near_loop(early + c * chunk, chunk, multiply(later_ref, early))

    def store(d):
        for k in range(2):
            keep_ref[d, k] = sums_ref[2 * d + k, pl.ds(4 * me, 4), :]
            give_ref[d, k] = sums_ref[2 * d + k, pl.ds(4 - 4 * me, 4), :]

    each(devices, store)


def far_kernel(
    every_ref, gather_ref, spread_ref, by_row_ref, by_col_ref,
    far_ref, left_ref, right_ref, lines_ref,
):
    devices = every_ref.shape[0]
    size, count = left_ref.shape
    sides = 8
    rank = size // sides

    lines = every_ref[:, 1].astype(f32).reshape(8 * devices, 128).astype(bf16)
    moments = dot(lines, gather_ref[...], FIRST)
    for h in range(2):
        left_ref[h * 128 : (h + 1) * 128, :] = moments[:, h * count : (h + 1) * count]
        right_ref[h * 128 : (h + 1) * 128, :] = moments[:, (2 + h) * count : (3 + h) * count]

    lines = []
    for h in range(2):
        total = 0.0
        for n, (matrix_ref, source_ref) in enumerate(((by_col_ref, right_ref), (by_row_ref, left_ref))):
            sums = [jnp.zeros((rank, count), f32) for _ in range(sides // 2)]
            for r in range(rank):
                matrix = matrix_ref[r * rank : (r + 1) * rank, :]
                for s in range(sides // 2):
                    at = h * 128 + s * rank + r
                    sums[s] = sums[s] + source_ref[at : at + 1, :] * matrix
            pair = jnp.concatenate(halves(jnp.concatenate(sums, axis=0)), axis=1)
            total = total + dot(pair, spread_ref[2 * n * count : (2 * n + 2) * count, :], PLAIN)
        lines.append(total)
    odd = lax.broadcasted_iota(jnp.int32, (128, 4 * devices), 1) % 2 == 1
    lines_ref[...] = jnp.where(odd, lines[1], lines[0]).T

    def store(d):
        far_ref[d, 0] = lines_ref[pl.ds(4 * d, 4), :]

    each(devices, store)

def join_kernel(far_ref, keep_ref, got_ref, out_hbm, near_ref, sems):
    far = start(far_ref, out_hbm.at[:, pl.ds(2, 1)], sems.at[0])
    near_ref[...] = keep_ref[...] + got_ref[...]
    near = start(near_ref, out_hbm.at[:, pl.ds(0, 2)], sems.at[1])
    far.wait()
    near.wait()


def direct_kernel(
    owner_hbm, col_hbm, row_hbm, blocks_hbm, every_ref, others_ref,
    out_ref, owner, col, row, blocks_ref, cells_ref, sems, *, inner,
):
    indices = start_indices(owner_hbm, col_hbm, row_hbm, owner, col, row, sems)
    copies = near_copies(blocks_hbm, 0, blocks_ref, EARLY + LATER, sems)
    chunk = blocks_ref.shape[0] // (EARLY + LATER)
    row_clusters = out_ref.shape[0]
    out_ref[...] = jnp.zeros(out_ref.shape, f32)
    me = lax.axis_index("col")

    def load(d):
        mine, other = every_ref[d, 0].astype(f32), others_ref[d, 0].astype(f32)
        first, second = jnp.where(me == 0, mine, other), jnp.where(me == 0, other, mine)
        for k in range(2):
            cells_ref[d, k] = jnp.concatenate([first[4 * k : 4 * k + 4], second[4 * k : 4 * k + 4]], axis=0)

    each(every_ref.shape[0], load)
    for copy in indices:
        copy.wait()

    def body(group):
        done = []
        for p in group:
            j = owner[0, p] * row_clusters + col[0, p]
            cells = cells_ref[slot_of(j, inner), j & 1].astype(bf16)
            done.append((row[0, p], dot(cells, blocks_ref[p], LAST)))
        for i, direct in done:
            out_ref[i] += direct

    for c, copy in enumerate(copies):
        copy.wait()
        near_loop(c * chunk, chunk, body)


def finish_kernel(parts_ref, mine_ref, other_ref, basis_ref, out_ref, *, inner):
    owned, rank, width = basis_ref.shape
    sides = out_ref.shape[0]
    depth = inner[0]
    near, far = [], jnp.zeros((4, 128), f32)
    for c in range(2):
        totals = (jnp.zeros((4, 128), f32), jnp.zeros((4, 128), f32), far)
        for x in range(inner[1]):

            def add(z, totals, first=(2 * x + c) * depth):
                return tuple(total + parts_ref[first + z, b] for b, total in enumerate(totals))

            totals = lax.fori_loop(0, depth, add, totals, unroll=min(8, depth))
        near.append(totals[:2])
        far = totals[2]
    me = lax.axis_index("col")
    mask = side_mask(sides, rank)
    for k in range(owned):
        total = jnp.concatenate([near[0][k], near[1][k]], axis=0)
        total = total + (mine_ref[2 * me + k] + other_ref[2 * me + k])
        flat = jnp.concatenate([far[2 * k : 2 * k + 1], far[2 * k + 1 : 2 * k + 2]], axis=1)
        high, low = halves(jnp.where(mask, flat, 0.0))
        tiled = jnp.concatenate([basis_ref[k]] * sides, axis=0)
        total = total + (dot(high, tiled, PLAIN) + dot(low, tiled, PLAIN))
        out_ref[:, k * width : (k + 1) * width] = total


def shards(cells, basis_t, near_blocks, near_owner, near_col, near_row, far_row, far_col, coupling):
    depth = lax.axis_size("z")
    inner = (depth, lax.axis_size("x"))
    devices = 2 * depth * inner[1]
    sides, lanes = cells.shape
    owned, rank, width = basis_t.shape
    row_clusters = owned * lax.axis_size("col")
    pairs = near_blocks.shape[0]
    count = coupling.shape[0]
    swap = [(0, 1), (1, 0)]
    params = pltpu.CompilerParams(vmem_limit_bytes=24 * 1024 * 1024)

    def shaped(shape, dtype):
        return jax.ShapeDtypeStruct(shape, dtype)

    def exchange(blocks):
        return lax.all_to_all(blocks, GROUP, split_axis=0, concat_axis=0, tiled=True)

    turn_cost = pl.CostEstimate(flops=10**6, bytes_accessed=3 * 10**6, transcendentals=0)
    near_cost = pl.CostEstimate(
        flops=2 * pairs * sides * width * width, bytes_accessed=10**7, transcendentals=0
    )
    payload = shaped((devices, 2, sides, 128), bf16)
    owner, column, line = [in_hbm(a.reshape(1, pairs)) for a in (near_owner, near_col, near_row)]
    first, second = [in_hbm(a.reshape(1, count)) for a in (far_row, far_col)]
    blocks = in_hbm(near_blocks)
    part = pairs // (EARLY + LATER)
    block = near_blocks.shape[1:]
    index_scratch = [pltpu.SMEM((1, pairs), jnp.int32)] * 3
    packed, mine, far, early_blocks = pl.pallas_call(
        lambda *refs: pack_kernel(*refs, inner=inner),
        out_shape=[
            payload,
            shaped(cells.shape, bf16),
            shaped((2, 1, count), jnp.int32),
            shaped((EARLY * part,) + block, bf16),
        ],
        in_specs=[HBM] * 5,
        out_specs=[HBM] + [VMEM] * 3,
        scratch_shapes=[
            pltpu.VMEM(cells.shape, bf16),
            pltpu.VMEM(basis_t.shape, bf16),
            pltpu.VMEM(payload.shape, bf16),
            pltpu.SemaphoreType.DMA((6,)),
        ],
        compiler_params=params,
        name="pack",
    )(in_hbm(cells), in_hbm(basis_t), first, second, blocks)
    every = exchange(packed)
    other = lax.ppermute(mine, "col", swap)
    by_row, by_col, gather, spread = pl.pallas_call(
        lambda *refs: turn_kernel(*refs, inner=inner),
        out_shape=[
            shaped((rank * rank, count), f32),
            shaped((rank * rank, count), f32),
            shaped((8 * devices, 4 * count), bf16),
            shaped((4 * count, 4 * devices), bf16),
        ],
        in_specs=[VMEM, HBM],
        out_specs=[VMEM] * 4,
        scratch_shapes=[pltpu.VMEM(coupling.shape, bf16), pltpu.SemaphoreType.DMA],
        compiler_params=params,
        cost_estimate=turn_cost,
        name="turn",
    )(far, in_hbm(coupling))
    keep, give = pl.pallas_call(
        lambda *refs: mirror_kernel(*refs, inner=inner),
        out_shape=[shaped((devices, 2, 4, 128), f32)] * 2,
        in_specs=[HBM] * 4 + [VMEM] * 4,
        out_specs=[VMEM] * 2,
        scratch_shapes=index_scratch
        + [
            pltpu.VMEM((LATER * part,) + block, bf16),
            pltpu.VMEM((row_clusters, sides, width), f32),
            pltpu.VMEM((2 * devices, sides, width), f32),
            pltpu.SemaphoreType.DMA((3 + LATER,)),
        ],
        compiler_params=params,
        cost_estimate=near_cost,
        name="mirror",
    )(owner, column, line, blocks, early_blocks, mine, other, spread)
    got = lax.ppermute(give, "col", swap)
    coupled = pl.pallas_call(
        far_kernel,
        out_shape=shaped((devices, 1, 4, 128), f32),
        in_specs=[VMEM] * 5,
        out_specs=VMEM,
        scratch_shapes=[pltpu.VMEM((sides * rank, count), f32)] * 2 + [pltpu.VMEM((4 * devices, 128), f32)],
        compiler_params=params,
        cost_estimate=turn_cost,
        name="far",
    )(every, gather, spread, by_row, by_col)
    partial = pl.pallas_call(
        join_kernel,
        out_shape=shaped((devices, 3, 4, 128), f32),
        in_specs=[VMEM] * 3,
        out_specs=HBM,
        scratch_shapes=[pltpu.VMEM(keep.shape, f32), pltpu.SemaphoreType.DMA((2,))],
        compiler_params=params,
        name="join",
    )(coupled, keep, got)
    parts = exchange(partial)
    every_other = lax.ppermute(every, "col", swap)
    direct = pl.pallas_call(
        lambda *refs: direct_kernel(*refs, inner=inner),
        out_shape=shaped((row_clusters, sides, width), f32),
        in_specs=[HBM] * 4 + [VMEM] * 2,
        out_specs=VMEM,
        scratch_shapes=index_scratch
        + [
            pltpu.VMEM(near_blocks.shape, bf16),
            pltpu.VMEM(payload.shape, f32),
            pltpu.SemaphoreType.DMA((3 + EARLY + LATER,)),
        ],
        compiler_params=params,
        cost_estimate=near_cost,
        name="direct",
    )(owner, column, line, blocks, every, every_other)
    others = lax.ppermute(direct, "col", swap)
    return pl.pallas_call(
        lambda *refs: finish_kernel(*refs, inner=inner),
        out_shape=shaped((sides, lanes), f32),
        in_specs=[VMEM] * 4,
        out_specs=VMEM,
        compiler_params=params,
        name="finish",
    )(parts, direct, others, basis_t)


def solution(mesh):
    parts, rows, cols = mesh.devices.shape
    x = 2 if rows % 2 == 0 else 1
    mesh = Mesh(mesh.devices.reshape(parts, rows // x, x, cols), ("parts", "z", "x", "col"))
    split = ("parts", "z", "x", "col")
    return jax.shard_map(
        shards,
        mesh=mesh,
        in_specs=(
            P(None, split),
            P(split, None, None),
            P(split, None, None),
            P(split, None),
            P(split, None),
            P(split, None),
            P(split, None),
            P(split, None),
            P(split, None),
        ),
        out_specs=P(None, split),
        check_vma=False,
    )
```

```python
import jax
import jax.numpy as jnp
from jax import lax
from jax.experimental import pallas as pl
from jax.experimental.pallas import tpu as pltpu
from jax.sharding import Mesh, PartitionSpec as P

f32 = jnp.float32
bf16 = jnp.bfloat16
LAST = (((1,), (1,)), ((), ()))
PLAIN = (((1,), (0,)), ((), ()))
FIRST = (((0,), (0,)), ((), ()))
HBM = pl.BlockSpec(memory_space=pltpu.HBM)
VMEM = pl.BlockSpec(memory_space=pltpu.VMEM)
EARLY, LATER = 1, 1
UNROLL = 48
GROUP = ("x", "col", "z")


def dot(left, right, dims):
    return lax.dot_general(left, right, dims, preferred_element_type=f32)


def halves(value):
    high = value.astype(bf16)
    return high, (value - high.astype(f32)).astype(bf16)


def one_hot(match):
    return match.astype(f32).astype(bf16)


def side_mask(sides, rank):
    row = lax.broadcasted_iota(jnp.int32, (sides, sides * rank), 0)
    lane = lax.broadcasted_iota(jnp.int32, (sides, sides * rank), 1)
    return lane // rank == row


def start(source, target, sem):
    copy = pltpu.make_async_copy(source, target, sem)
    copy.start()
    return copy


def in_hbm(array):
    return pltpu.with_memory_space_constraint(array, pltpu.HBM)


def slot_of(cluster, inner):
    depth, width = inner
    device = cluster >> 1
    return lax.rem(device, 2 * width) * depth + lax.div(device, 2 * width)


def each(count, body):
    if count <= 16:
        for d in range(count):
            body(d)
    else:
        pl.loop(0, count)(body)


def pack_kernel(
    cells_hbm, basis_hbm, first_hbm, second_hbm, coupling_hbm, blocks_hbm,
    out_hbm, mine_ref, far_ref, coupling_ref, early_ref,
    cells_ref, basis_ref, out_ref, sems, *, inner,
):
    copies = [
        start(cells_hbm, cells_ref, sems.at[0]),
        start(basis_hbm, basis_ref, sems.at[1]),
    ]
    ahead = [
        start(first_hbm, far_ref.at[0], sems.at[2]),
        start(second_hbm, far_ref.at[1], sems.at[3]),
        start(coupling_hbm, coupling_ref, sems.at[4]),
        start(blocks_hbm.at[pl.ds(0, early_ref.shape[0])], early_ref, sems.at[5]),
    ]
    sides = cells_ref.shape[0]
    owned, rank, width = basis_ref.shape
    mask = side_mask(sides, rank)
    for copy in copies:
        copy.wait()
    mine_ref[...] = cells_ref[...]
    blocks, lines = [], []
    for k in range(owned):
        cells = cells_ref[:, k * width : (k + 1) * width]
        blocks.append(cells.astype(f32))
        tiled = jnp.concatenate([basis_ref[k]] * sides, axis=0)
        every = dot(cells, tiled, LAST)
        flat = jnp.sum(jnp.where(mask, every, 0.0), axis=0, keepdims=True)
        lines += [flat[:, :128], flat[:, 128:]]
    moments = jnp.concatenate(lines, axis=0)
    high = moments.astype(bf16).astype(f32)
    moments = jnp.concatenate([high, moments - high], axis=0).astype(bf16)
    for c in range(2):
        half = jnp.concatenate([block[4 * c : 4 * c + 4] for block in blocks], axis=0).astype(bf16)
        for x in range(inner[1]):

            def store(z, c=c, x=x, half=half):
                d = (2 * x + c) * inner[0] + z
                out_ref[d, 0] = half
                out_ref[d, 1] = moments

            each(inner[0], store)
    start(out_ref, out_hbm, sems.at[0]).wait()
    for copy in ahead:
        copy.wait()


def start_indices(owner_hbm, col_hbm, row_hbm, owner, col, row, sems):
    return [
        start(owner_hbm, owner, sems.at[0]),
        start(col_hbm, col, sems.at[1]),
        start(row_hbm, row, sems.at[2]),
    ]


def near_copies(blocks_hbm, first, blocks_ref, chunks, sems):
    size = blocks_ref.shape[0] // chunks
    return [
        start(blocks_hbm.at[pl.ds(first + c * size, size)], blocks_ref.at[pl.ds(c * size, size)], sems.at[3 + c])
        for c in range(chunks)
    ]


def near_loop(first, size, body):
    unroll = min(UNROLL, size)

    def group(g, _):
        body([first + g * unroll + u for u in range(unroll)])
        return 0

    lax.fori_loop(0, size // unroll, group, 0)


def turn_kernel(
    far, coupling_ref, by_row_ref, by_col_ref, gather_ref, spread_ref, *, inner
):
    count, size = coupling_ref.shape
    rank = round(size**0.5)
    devices = gather_ref.shape[0] // 8
    source = lax.broadcasted_iota(jnp.int32, (8 * devices, count), 0)
    target = lax.broadcasted_iota(jnp.int32, (4 * devices, count), 0)
    for n in range(2):
        c = far[n]
        slot, k = slot_of(c, inner), c & 1
        for h in range(2):
            at = 8 * slot + 2 * k + h
            hot = one_hot((source == at) | (source == at + 4))
            gather_ref[:, (2 * n + h) * count : (2 * n + h + 1) * count] = hot
        at = 4 * slot + 2 * k
        hot = ((target == at) | (target == at + 1)).astype(f32).T.astype(bf16)
        spread_ref[2 * n * count : (2 * n + 1) * count, :] = hot
        spread_ref[(2 * n + 1) * count : (2 * n + 2) * count, :] = hot

    for t in range(0, size, 128):
        by_row_ref[t : t + 128, :] = coupling_ref[:, t : t + 128].astype(f32).T
    for k in range(rank):
        by_col_ref[k * rank : (k + 1) * rank, :] = by_row_ref[pl.ds(k, rank, stride=rank), :]


def mirror_kernel(
    owner_hbm, col_hbm, row_hbm, blocks_hbm, early_ref, mine_ref, other_ref,
    keep_ref, give_ref,
    owner, col, row, later_ref, cells_ref, sums_ref, sems, *, inner,
):
    early, width, _ = early_ref.shape
    chunk = early // EARLY
    indices = start_indices(owner_hbm, col_hbm, row_hbm, owner, col, row, sems)
    copies = near_copies(blocks_hbm, early, later_ref, LATER, sems)
    devices = keep_ref.shape[0]
    row_clusters = cells_ref.shape[0]
    me = lax.axis_index("col")
    for k in range(2):
        cells_ref[2 * me + k] = mine_ref[:, k * width : (k + 1) * width].astype(f32)
        cells_ref[2 - 2 * me + k] = other_ref[:, k * width : (k + 1) * width].astype(f32)
    sums_ref[...] = jnp.zeros(sums_ref.shape, f32)

    def multiply(source_ref, first):
        def body(group):
            done = []
            for p in group:
                j = owner[0, p] * row_clusters + col[0, p]
                at = 2 * slot_of(j, inner) + (j & 1)
                cells = cells_ref[row[0, p]].astype(bf16)
                done.append((at, dot(cells, source_ref[p - first], PLAIN)))
            for at, mirrored in done:
                sums_ref[at] += mirrored

        return body

    for copy in indices:
        copy.wait()
    near_loop(0, early, multiply(early_ref, 0))
    for c, copy in enumerate(copies):
        copy.wait()
        near_loop(early + c * chunk, chunk, multiply(later_ref, early))

    def store(d):
        for k in range(2):
            keep_ref[d, k] = sums_ref[2 * d + k, pl.ds(4 * me, 4), :]
            give_ref[d, k] = sums_ref[2 * d + k, pl.ds(4 - 4 * me, 4), :]

    each(devices, store)


def far_kernel(
    every_ref, gather_ref, spread_ref, by_row_ref, by_col_ref,
    far_ref, left_ref, right_ref, lines_ref,
):
    devices = every_ref.shape[0]
    size, count = left_ref.shape
    sides = 8
    rank = size // sides

    lines = every_ref[:, 1].reshape(8 * devices, 128)
    moments = dot(lines, gather_ref[...], FIRST)
    for h in range(2):
        left_ref[h * 128 : (h + 1) * 128, :] = moments[:, h * count : (h + 1) * count]
        right_ref[h * 128 : (h + 1) * 128, :] = moments[:, (2 + h) * count : (3 + h) * count]

    lines = []
    for h in range(2):
        total = 0.0
        for n, (matrix_ref, source_ref) in enumerate(((by_col_ref, right_ref), (by_row_ref, left_ref))):
            sums = [jnp.zeros((rank, count), f32) for _ in range(sides // 2)]
            for r in range(rank):
                matrix = matrix_ref[r * rank : (r + 1) * rank, :]
                for s in range(sides // 2):
                    at = h * 128 + s * rank + r
                    sums[s] = sums[s] + source_ref[at : at + 1, :] * matrix
            pair = jnp.concatenate(halves(jnp.concatenate(sums, axis=0)), axis=1)
            total = total + dot(pair, spread_ref[2 * n * count : (2 * n + 2) * count, :], PLAIN)
        lines.append(total)
    odd = lax.broadcasted_iota(jnp.int32, (128, 4 * devices), 1) % 2 == 1
    lines_ref[...] = jnp.where(odd, lines[1], lines[0]).T

    def store(d):
        far_ref[d, 0] = lines_ref[pl.ds(4 * d, 4), :]

    each(devices, store)

def join_kernel(far_ref, keep_ref, got_ref, out_hbm, near_ref, sems):
    far = start(far_ref, out_hbm.at[:, pl.ds(2, 1)], sems.at[0])
    near_ref[...] = keep_ref[...] + got_ref[...]
    near = start(near_ref, out_hbm.at[:, pl.ds(0, 2)], sems.at[1])
    far.wait()
    near.wait()


def direct_kernel(
    owner_hbm, col_hbm, row_hbm, blocks_hbm, every_ref, others_ref,
    out_ref, owner, col, row, blocks_ref, cells_ref, sems, *, inner,
):
    indices = start_indices(owner_hbm, col_hbm, row_hbm, owner, col, row, sems)
    copies = near_copies(blocks_hbm, 0, blocks_ref, EARLY + LATER, sems)
    chunk = blocks_ref.shape[0] // (EARLY + LATER)
    row_clusters = out_ref.shape[0]
    out_ref[...] = jnp.zeros(out_ref.shape, f32)
    me = lax.axis_index("col")

    def load(d):
        mine, other = every_ref[d, 0].astype(f32), others_ref[d, 0].astype(f32)
        first, second = jnp.where(me == 0, mine, other), jnp.where(me == 0, other, mine)
        for k in range(2):
            cells_ref[d, k] = jnp.concatenate([first[4 * k : 4 * k + 4], second[4 * k : 4 * k + 4]], axis=0)

    each(every_ref.shape[0], load)
    for copy in indices:
        copy.wait()

    def body(group):
        done = []
        for p in group:
            j = owner[0, p] * row_clusters + col[0, p]
            cells = cells_ref[slot_of(j, inner), j & 1].astype(bf16)
            done.append((row[0, p], dot(cells, blocks_ref[p], LAST)))
        for i, direct in done:
            out_ref[i] += direct

    for c, copy in enumerate(copies):
        copy.wait()
        near_loop(c * chunk, chunk, body)


def finish_kernel(parts_ref, mine_ref, other_ref, basis_ref, out_ref, *, inner):
    owned, rank, width = basis_ref.shape
    sides = out_ref.shape[0]
    depth = inner[0]
    near, far = [], jnp.zeros((4, 128), f32)
    for c in range(2):
        totals = (jnp.zeros((4, 128), f32), jnp.zeros((4, 128), f32), far)
        for x in range(inner[1]):

            def add(z, totals, first=(2 * x + c) * depth):
                return tuple(total + parts_ref[first + z, b] for b, total in enumerate(totals))

            totals = lax.fori_loop(0, depth, add, totals, unroll=min(8, depth))
        near.append(totals[:2])
        far = totals[2]
    me = lax.axis_index("col")
    mask = side_mask(sides, rank)
    for k in range(owned):
        total = jnp.concatenate([near[0][k], near[1][k]], axis=0)
        total = total + (mine_ref[2 * me + k] + other_ref[2 * me + k])
        flat = jnp.concatenate([far[2 * k : 2 * k + 1], far[2 * k + 1 : 2 * k + 2]], axis=1)
        high, low = halves(jnp.where(mask, flat, 0.0))
        tiled = jnp.concatenate([basis_ref[k]] * sides, axis=0)
        both = dot(jnp.concatenate([high, low], axis=0), tiled, PLAIN)
        total = total + (both[:sides] + both[sides:])
        out_ref[:, k * width : (k + 1) * width] = total


def shards(cells, basis_t, near_blocks, near_owner, near_col, near_row, far_row, far_col, coupling):
    depth = lax.axis_size("z")
    inner = (depth, lax.axis_size("x"))
    devices = 2 * depth * inner[1]
    sides, lanes = cells.shape
    owned, rank, width = basis_t.shape
    row_clusters = owned * lax.axis_size("col")
    pairs = near_blocks.shape[0]
    count = coupling.shape[0]
    swap = [(0, 1), (1, 0)]
    params = pltpu.CompilerParams(vmem_limit_bytes=12 * 1024 * 1024)

    def shaped(shape, dtype):
        return jax.ShapeDtypeStruct(shape, dtype)

    def exchange(blocks):
        return lax.all_to_all(blocks, GROUP, split_axis=0, concat_axis=0, tiled=True)

    turn_cost = pl.CostEstimate(flops=10**6, bytes_accessed=3 * 10**6, transcendentals=0)
    near_cost = pl.CostEstimate(
        flops=2 * pairs * sides * width * width, bytes_accessed=10**7, transcendentals=0
    )
    payload = shaped((devices, 2, sides, 128), bf16)
    owner, column, line = [in_hbm(a.reshape(1, pairs)) for a in (near_owner, near_col, near_row)]
    first, second = [in_hbm(a.reshape(1, count)) for a in (far_row, far_col)]
    blocks = in_hbm(near_blocks)
    part = pairs // (EARLY + LATER)
    block = near_blocks.shape[1:]
    index_scratch = [pltpu.SMEM((1, pairs), jnp.int32)] * 3
    packed, mine, far, couplings, early_blocks = pl.pallas_call(
        lambda *refs: pack_kernel(*refs, inner=inner),
        out_shape=[
            payload,
            shaped(cells.shape, bf16),
            shaped((2, 1, count), jnp.int32),
            shaped(coupling.shape, bf16),
            shaped((EARLY * part,) + block, bf16),
        ],
        in_specs=[HBM] * 6,
        out_specs=[HBM] + [VMEM] * 4,
        scratch_shapes=[
            pltpu.VMEM(cells.shape, bf16),
            pltpu.VMEM(basis_t.shape, bf16),
            pltpu.VMEM(payload.shape, bf16),
            pltpu.SemaphoreType.DMA((6,)),
        ],
        compiler_params=params,
        name="pack",
    )(in_hbm(cells), in_hbm(basis_t), first, second, in_hbm(coupling), blocks)
    every = exchange(packed)
    other = lax.ppermute(mine, "col", swap)
    by_row, by_col, gather, spread = pl.pallas_call(
        lambda *refs: turn_kernel(*refs, inner=inner),
        out_shape=[
            shaped((rank * rank, count), f32),
            shaped((rank * rank, count), f32),
            shaped((8 * devices, 4 * count), bf16),
            shaped((4 * count, 4 * devices), bf16),
        ],
        in_specs=[VMEM] * 2,
        out_specs=[VMEM] * 4,
        compiler_params=params,
        cost_estimate=turn_cost,
        name="turn",
    )(far, couplings)
    keep, give = pl.pallas_call(
        lambda *refs: mirror_kernel(*refs, inner=inner),
        out_shape=[shaped((devices, 2, 4, 128), f32)] * 2,
        in_specs=[HBM] * 4 + [VMEM] * 3,
        out_specs=[VMEM] * 2,
        scratch_shapes=index_scratch
        + [
            pltpu.VMEM((LATER * part,) + block, bf16),
            pltpu.VMEM((row_clusters, sides, width), f32),
            pltpu.VMEM((2 * devices, sides, width), f32),
            pltpu.SemaphoreType.DMA((3 + LATER,)),
        ],
        compiler_params=params,
        cost_estimate=near_cost,
        name="mirror",
    )(owner, column, line, blocks, early_blocks, mine, other)
    got = lax.ppermute(give, "col", swap)
    coupled = pl.pallas_call(
        far_kernel,
        out_shape=shaped((devices, 1, 4, 128), f32),
        in_specs=[VMEM] * 5,
        out_specs=VMEM,
        scratch_shapes=[pltpu.VMEM((sides * rank, count), f32)] * 2 + [pltpu.VMEM((4 * devices, 128), f32)],
        compiler_params=params,
        cost_estimate=turn_cost,
        name="far",
    )(every, gather, spread, by_row, by_col)
    partial = pl.pallas_call(
        join_kernel,
        out_shape=shaped((devices, 3, 4, 128), f32),
        in_specs=[VMEM] * 3,
        out_specs=HBM,
        scratch_shapes=[pltpu.VMEM(keep.shape, f32), pltpu.SemaphoreType.DMA((2,))],
        compiler_params=params,
        name="join",
    )(coupled, keep, got)
    parts = exchange(partial)
    every_other = lax.ppermute(every, "col", swap)
    direct = pl.pallas_call(
        lambda *refs: direct_kernel(*refs, inner=inner),
        out_shape=shaped((row_clusters, sides, width), f32),
        in_specs=[HBM] * 4 + [VMEM] * 2,
        out_specs=VMEM,
        scratch_shapes=index_scratch
        + [
            pltpu.VMEM(near_blocks.shape, bf16),
            pltpu.VMEM(payload.shape, f32),
            pltpu.SemaphoreType.DMA((3 + EARLY + LATER,)),
        ],
        compiler_params=params,
        cost_estimate=near_cost,
        name="direct",
    )(owner, column, line, blocks, every, every_other)
    others = lax.ppermute(direct, "col", swap)
    return pl.pallas_call(
        lambda *refs: finish_kernel(*refs, inner=inner),
        out_shape=shaped((sides, lanes), f32),
        in_specs=[VMEM] * 4,
        out_specs=VMEM,
        compiler_params=params,
        name="finish",
    )(parts, direct, others, basis_t)


def solution(mesh):
    parts, rows, cols = mesh.devices.shape
    x = 2 if rows % 2 == 0 else 1
    mesh = Mesh(mesh.devices.reshape(parts, rows // x, x, cols), ("parts", "z", "x", "col"))
    split = ("parts", "z", "x", "col")
    return jax.shard_map(
        shards,
        mesh=mesh,
        in_specs=(
            P(None, split),
            P(split, None, None),
            P(split, None, None),
            P(split, None),
            P(split, None),
            P(split, None),
            P(split, None),
            P(split, None),
            P(split, None),
        ),
        out_specs=P(None, split),
        check_vma=False,
    )
```

```python
import jax
import jax.numpy as jnp
from jax import lax
from jax.experimental import pallas as pl
from jax.experimental.pallas import tpu as pltpu
from jax.sharding import Mesh, PartitionSpec as P

f32 = jnp.float32
bf16 = jnp.bfloat16
LAST = (((1,), (1,)), ((), ()))
PLAIN = (((1,), (0,)), ((), ()))
FIRST = (((0,), (0,)), ((), ()))
HBM = pl.BlockSpec(memory_space=pltpu.HBM)
VMEM = pl.BlockSpec(memory_space=pltpu.VMEM)
EARLY, LATER = 1, 1
UNROLL = 48
GROUP = ('w', 'x', 'col', 'z')


def dot(left, right, dims):
    return lax.dot_general(left, right, dims, preferred_element_type=f32)


def halves(value):
    high = value.astype(bf16)
    return high, (value - high.astype(f32)).astype(bf16)


def one_hot(match):
    return match.astype(f32).astype(bf16)


def side_mask(sides, rank):
    row = lax.broadcasted_iota(jnp.int32, (sides, sides * rank), 0)
    lane = lax.broadcasted_iota(jnp.int32, (sides, sides * rank), 1)
    return lane // rank == row


def start(source, target, sem):
    copy = pltpu.make_async_copy(source, target, sem)
    copy.start()
    return copy


def in_hbm(array):
    return pltpu.with_memory_space_constraint(array, pltpu.HBM)


def slot_of(cluster, inner):
    depth, _, width, depth_z, depth_w = inner
    device = cluster >> 1
    c, device = device & 1, device >> 1
    x, device = lax.rem(device, width), lax.div(device, width)
    z, w = lax.rem(device, depth_z), lax.div(device, depth_z)
    return (((w) * width + x) * 2 + c) * depth + (z)


def each(count, body):
    if count <= 16:
        for d in range(count):
            body(d)
    else:
        pl.loop(0, count)(body)


def pack_kernel(
    cells_hbm, basis_hbm, first_hbm, second_hbm, coupling_hbm, blocks_hbm,
    out_hbm, mine_ref, far_ref, coupling_ref, early_ref,
    cells_ref, basis_ref, out_ref, sems, *, inner,
):
    copies = [
        start(cells_hbm, cells_ref, sems.at[0]),
        start(basis_hbm, basis_ref, sems.at[1]),
    ]
    ahead = [
        start(first_hbm, far_ref.at[0], sems.at[2]),
        start(second_hbm, far_ref.at[1], sems.at[3]),
        start(coupling_hbm, coupling_ref, sems.at[4]),
        start(blocks_hbm.at[pl.ds(0, early_ref.shape[0])], early_ref, sems.at[5]),
    ]
    sides = cells_ref.shape[0]
    owned, rank, width = basis_ref.shape
    mask = side_mask(sides, rank)
    for copy in copies:
        copy.wait()
    mine_ref[...] = cells_ref[...]
    blocks, lines = [], []
    for k in range(owned):
        cells = cells_ref[:, k * width : (k + 1) * width]
        blocks.append(cells.astype(f32))
        tiled = jnp.concatenate([basis_ref[k]] * sides, axis=0)
        every = dot(cells, tiled, LAST)
        flat = jnp.sum(jnp.where(mask, every, 0.0), axis=0, keepdims=True)
        lines += [flat[:, :128], flat[:, 128:]]
    moments = jnp.concatenate(lines, axis=0)
    high = moments.astype(bf16).astype(f32)
    moments = jnp.concatenate([high, moments - high], axis=0).astype(bf16)
    for c in range(2):
        half = jnp.concatenate([block[4 * c : 4 * c + 4] for block in blocks], axis=0).astype(bf16)
        for x in range(inner[1]):

            def store(z, c=c, x=x, half=half):
                d = (2 * x + c) * inner[0] + z
                out_ref[d, 0] = half
                out_ref[d, 1] = moments

            each(inner[0], store)
    start(out_ref, out_hbm, sems.at[0]).wait()
    for copy in ahead:
        copy.wait()


def start_indices(owner_hbm, col_hbm, row_hbm, owner, col, row, sems):
    return [
        start(owner_hbm, owner, sems.at[0]),
        start(col_hbm, col, sems.at[1]),
        start(row_hbm, row, sems.at[2]),
    ]


def near_copies(blocks_hbm, first, blocks_ref, chunks, sems):
    size = blocks_ref.shape[0] // chunks
    return [
        start(blocks_hbm.at[pl.ds(first + c * size, size)], blocks_ref.at[pl.ds(c * size, size)], sems.at[3 + c])
        for c in range(chunks)
    ]


def near_loop(first, size, body):
    unroll = min(UNROLL, size)

    def group(g, _):
        body([first + g * unroll + u for u in range(unroll)])
        return 0

    lax.fori_loop(0, size // unroll, group, 0)


def turn_kernel(
    far, coupling_ref, by_row_ref, by_col_ref, gather_ref, spread_ref, *, inner
):
    count, size = coupling_ref.shape
    rank = round(size**0.5)
    devices = gather_ref.shape[0] // 8
    source = lax.broadcasted_iota(jnp.int32, (8 * devices, count), 0)
    target = lax.broadcasted_iota(jnp.int32, (4 * devices, count), 0)
    for n in range(2):
        c = far[n]
        slot, k = slot_of(c, inner), c & 1
        for h in range(2):
            at = 8 * slot + 2 * k + h
            hot = one_hot((source == at) | (source == at + 4))
            gather_ref[:, (2 * n + h) * count : (2 * n + h + 1) * count] = hot
        at = 4 * slot + 2 * k
        hot = ((target == at) | (target == at + 1)).astype(f32).T.astype(bf16)
        spread_ref[2 * n * count : (2 * n + 1) * count, :] = hot
        spread_ref[(2 * n + 1) * count : (2 * n + 2) * count, :] = hot

    for t in range(0, size, 128):
        by_row_ref[t : t + 128, :] = coupling_ref[:, t : t + 128].astype(f32).T
    for k in range(rank):
        by_col_ref[k * rank : (k + 1) * rank, :] = by_row_ref[pl.ds(k, rank, stride=rank), :]


def mirror_kernel(
    owner_hbm, col_hbm, row_hbm, blocks_hbm, early_ref, mine_ref, other_ref,
    keep_ref, give_ref,
    owner, col, row, later_ref, cells_ref, sums_ref, sems, *, inner,
):
    early, width, _ = early_ref.shape
    chunk = early // EARLY
    indices = start_indices(owner_hbm, col_hbm, row_hbm, owner, col, row, sems)
    copies = near_copies(blocks_hbm, early, later_ref, LATER, sems)
    devices = keep_ref.shape[0]
    row_clusters = cells_ref.shape[0]
    me = lax.axis_index("col")
    for k in range(2):
        cells_ref[2 * me + k] = mine_ref[:, k * width : (k + 1) * width].astype(f32)
        cells_ref[2 - 2 * me + k] = other_ref[:, k * width : (k + 1) * width].astype(f32)
    sums_ref[...] = jnp.zeros(sums_ref.shape, f32)

    def multiply(source_ref, first):
        def body(group):
            done = []
            for p in group:
                j = owner[0, p] * row_clusters + col[0, p]
                at = 2 * slot_of(j, inner) + (j & 1)
                cells = cells_ref[row[0, p]].astype(bf16)
                done.append((at, dot(cells, source_ref[p - first], PLAIN)))
            for at, mirrored in done:
                sums_ref[at] += mirrored

        return body

    for copy in indices:
        copy.wait()
    near_loop(0, early, multiply(early_ref, 0))
    for c, copy in enumerate(copies):
        copy.wait()
        near_loop(early + c * chunk, chunk, multiply(later_ref, early))

    def store(d):
        for k in range(2):
            keep_ref[d, k] = sums_ref[2 * d + k, pl.ds(4 * me, 4), :]
            give_ref[d, k] = sums_ref[2 * d + k, pl.ds(4 - 4 * me, 4), :]

    each(devices, store)


def far_kernel(
    every_ref, gather_ref, spread_ref, by_row_ref, by_col_ref,
    far_ref, left_ref, right_ref, lines_ref,
):
    devices = every_ref.shape[0]
    size, count = left_ref.shape
    sides = 8
    rank = size // sides

    lines = every_ref[:, 1].astype(f32).reshape(8 * devices, 128).astype(bf16)
    moments = dot(lines, gather_ref[...], FIRST)
    for h in range(2):
        left_ref[h * 128 : (h + 1) * 128, :] = moments[:, h * count : (h + 1) * count]
        right_ref[h * 128 : (h + 1) * 128, :] = moments[:, (2 + h) * count : (3 + h) * count]

    lines = []
    for h in range(2):
        total = 0.0
        for n, (matrix_ref, source_ref) in enumerate(((by_col_ref, right_ref), (by_row_ref, left_ref))):
            sums = [jnp.zeros((rank, count), f32) for _ in range(sides // 2)]
            for r in range(rank):
                matrix = matrix_ref[r * rank : (r + 1) * rank, :]
                for s in range(sides // 2):
                    at = h * 128 + s * rank + r
                    sums[s] = sums[s] + source_ref[at : at + 1, :] * matrix
            pair = jnp.concatenate(halves(jnp.concatenate(sums, axis=0)), axis=1)
            total = total + dot(pair, spread_ref[2 * n * count : (2 * n + 2) * count, :], PLAIN)
        lines.append(total)
    odd = lax.broadcasted_iota(jnp.int32, (128, 4 * devices), 1) % 2 == 1
    lines_ref[...] = jnp.where(odd, lines[1], lines[0]).T

    def store(d):
        far_ref[d, 0] = lines_ref[pl.ds(4 * d, 4), :]

    each(devices, store)

def join_kernel(far_ref, keep_ref, got_ref, out_hbm, near_ref, sems):
    far = start(far_ref, out_hbm.at[:, pl.ds(2, 1)], sems.at[0])
    near_ref[...] = keep_ref[...] + got_ref[...]
    near = start(near_ref, out_hbm.at[:, pl.ds(0, 2)], sems.at[1])
    far.wait()
    near.wait()


def direct_kernel(
    owner_hbm, col_hbm, row_hbm, blocks_hbm, every_ref, others_ref,
    out_ref, owner, col, row, blocks_ref, cells_ref, sems, *, inner,
):
    indices = start_indices(owner_hbm, col_hbm, row_hbm, owner, col, row, sems)
    copies = near_copies(blocks_hbm, 0, blocks_ref, EARLY + LATER, sems)
    chunk = blocks_ref.shape[0] // (EARLY + LATER)
    row_clusters = out_ref.shape[0]
    out_ref[...] = jnp.zeros(out_ref.shape, f32)
    me = lax.axis_index("col")

    def load(d):
        mine, other = every_ref[d, 0].astype(f32), others_ref[d, 0].astype(f32)
        first, second = jnp.where(me == 0, mine, other), jnp.where(me == 0, other, mine)
        for k in range(2):
            cells_ref[d, k] = jnp.concatenate([first[4 * k : 4 * k + 4], second[4 * k : 4 * k + 4]], axis=0)

    each(every_ref.shape[0], load)
    for copy in indices:
        copy.wait()

    def body(group):
        done = []
        for p in group:
            j = owner[0, p] * row_clusters + col[0, p]
            cells = cells_ref[slot_of(j, inner), j & 1].astype(bf16)
            done.append((row[0, p], dot(cells, blocks_ref[p], LAST)))
        for i, direct in done:
            out_ref[i] += direct

    for c, copy in enumerate(copies):
        copy.wait()
        near_loop(c * chunk, chunk, body)


def finish_kernel(parts_ref, mine_ref, other_ref, basis_ref, out_ref, *, inner):
    owned, rank, width = basis_ref.shape
    sides = out_ref.shape[0]
    depth = inner[0]
    near, far = [], jnp.zeros((4, 128), f32)
    for c in range(2):
        totals = (jnp.zeros((4, 128), f32), jnp.zeros((4, 128), f32), far)
        for x in range(inner[1]):

            def add(z, totals, first=(2 * x + c) * depth):
                return tuple(total + parts_ref[first + z, b] for b, total in enumerate(totals))

            totals = lax.fori_loop(0, depth, add, totals, unroll=min(8, depth))
        near.append(totals[:2])
        far = totals[2]
    me = lax.axis_index("col")
    mask = side_mask(sides, rank)
    for k in range(owned):
        total = jnp.concatenate([near[0][k], near[1][k]], axis=0)
        total = total + (mine_ref[2 * me + k] + other_ref[2 * me + k])
        flat = jnp.concatenate([far[2 * k : 2 * k + 1], far[2 * k + 1 : 2 * k + 2]], axis=1)
        high, low = halves(jnp.where(mask, flat, 0.0))
        tiled = jnp.concatenate([basis_ref[k]] * sides, axis=0)
        total = total + (dot(high, tiled, PLAIN) + dot(low, tiled, PLAIN))
        out_ref[:, k * width : (k + 1) * width] = total


def shards(cells, basis_t, near_blocks, near_owner, near_col, near_row, far_row, far_col, coupling):
    depth = lax.axis_size("z")
    inner = (depth, lax.axis_size("w") * lax.axis_size("x"), lax.axis_size("x"), lax.axis_size("z"), lax.axis_size("w"))
    devices = 2 * depth * inner[1]
    sides, lanes = cells.shape
    owned, rank, width = basis_t.shape
    row_clusters = owned * lax.axis_size("col")
    pairs = near_blocks.shape[0]
    count = coupling.shape[0]
    swap = [(0, 1), (1, 0)]
    params = pltpu.CompilerParams(vmem_limit_bytes=24 * 1024 * 1024)

    def shaped(shape, dtype):
        return jax.ShapeDtypeStruct(shape, dtype)

    def exchange(blocks):
        return lax.all_to_all(blocks, GROUP, split_axis=0, concat_axis=0, tiled=True)

    turn_cost = pl.CostEstimate(flops=10**6, bytes_accessed=3 * 10**6, transcendentals=0)
    near_cost = pl.CostEstimate(
        flops=2 * pairs * sides * width * width, bytes_accessed=10**7, transcendentals=0
    )
    payload = shaped((devices, 2, sides, 128), bf16)
    owner, column, line = [in_hbm(a.reshape(1, pairs)) for a in (near_owner, near_col, near_row)]
    first, second = [in_hbm(a.reshape(1, count)) for a in (far_row, far_col)]
    blocks = in_hbm(near_blocks)
    part = pairs // (EARLY + LATER)
    block = near_blocks.shape[1:]
    index_scratch = [pltpu.SMEM((1, pairs), jnp.int32)] * 3
    packed, mine, far, couplings, early_blocks = pl.pallas_call(
        lambda *refs: pack_kernel(*refs, inner=inner),
        out_shape=[
            payload,
            shaped(cells.shape, bf16),
            shaped((2, 1, count), jnp.int32),
            shaped(coupling.shape, bf16),
            shaped((EARLY * part,) + block, bf16),
        ],
        in_specs=[HBM] * 6,
        out_specs=[HBM] + [VMEM] * 4,
        scratch_shapes=[
            pltpu.VMEM(cells.shape, bf16),
            pltpu.VMEM(basis_t.shape, bf16),
            pltpu.VMEM(payload.shape, bf16),
            pltpu.SemaphoreType.DMA((6,)),
        ],
        compiler_params=params,
        name="pack",
    )(in_hbm(cells), in_hbm(basis_t), first, second, in_hbm(coupling), blocks)
    every = exchange(packed)
    other = lax.ppermute(mine, "col", swap)
    by_row, by_col, gather, spread = pl.pallas_call(
        lambda *refs: turn_kernel(*refs, inner=inner),
        out_shape=[
            shaped((rank * rank, count), f32),
            shaped((rank * rank, count), f32),
            shaped((8 * devices, 4 * count), bf16),
            shaped((4 * count, 4 * devices), bf16),
        ],
        in_specs=[VMEM] * 2,
        out_specs=[VMEM] * 4,
        compiler_params=params,
        cost_estimate=turn_cost,
        name="turn",
    )(far, couplings)
    keep, give = pl.pallas_call(
        lambda *refs: mirror_kernel(*refs, inner=inner),
        out_shape=[shaped((devices, 2, 4, 128), f32)] * 2,
        in_specs=[HBM] * 4 + [VMEM] * 3,
        out_specs=[VMEM] * 2,
        scratch_shapes=index_scratch
        + [
            pltpu.VMEM((LATER * part,) + block, bf16),
            pltpu.VMEM((row_clusters, sides, width), f32),
            pltpu.VMEM((2 * devices, sides, width), f32),
            pltpu.SemaphoreType.DMA((3 + LATER,)),
        ],
        compiler_params=params,
        cost_estimate=near_cost,
        name="mirror",
    )(owner, column, line, blocks, early_blocks, mine, other)
    got = lax.ppermute(give, "col", swap)
    coupled = pl.pallas_call(
        far_kernel,
        out_shape=shaped((devices, 1, 4, 128), f32),
        in_specs=[VMEM] * 5,
        out_specs=VMEM,
        scratch_shapes=[pltpu.VMEM((sides * rank, count), f32)] * 2 + [pltpu.VMEM((4 * devices, 128), f32)],
        compiler_params=params,
        cost_estimate=turn_cost,
        name="far",
    )(every, gather, spread, by_row, by_col)
    partial = pl.pallas_call(
        join_kernel,
        out_shape=shaped((devices, 3, 4, 128), f32),
        in_specs=[VMEM] * 3,
        out_specs=HBM,
        scratch_shapes=[pltpu.VMEM(keep.shape, f32), pltpu.SemaphoreType.DMA((2,))],
        compiler_params=params,
        name="join",
    )(coupled, keep, got)
    parts = exchange(partial)
    every_other = lax.ppermute(every, "col", swap)
    direct = pl.pallas_call(
        lambda *refs: direct_kernel(*refs, inner=inner),
        out_shape=shaped((row_clusters, sides, width), f32),
        in_specs=[HBM] * 4 + [VMEM] * 2,
        out_specs=VMEM,
        scratch_shapes=index_scratch
        + [
            pltpu.VMEM(near_blocks.shape, bf16),
            pltpu.VMEM(payload.shape, f32),
            pltpu.SemaphoreType.DMA((3 + EARLY + LATER,)),
        ],
        compiler_params=params,
        cost_estimate=near_cost,
        name="direct",
    )(owner, column, line, blocks, every, every_other)
    others = lax.ppermute(direct, "col", swap)
    return pl.pallas_call(
        lambda *refs: finish_kernel(*refs, inner=inner),
        out_shape=shaped((sides, lanes), f32),
        in_specs=[VMEM] * 4,
        out_specs=VMEM,
        compiler_params=params,
        name="finish",
    )(parts, direct, others, basis_t)


def solution(mesh):
    parts, rows, cols = mesh.devices.shape
    x = 2 if rows % 2 == 0 else 1
    w = 2 if rows // x % 2 == 0 else 1
    mesh = Mesh(mesh.devices.reshape(parts, w, rows // x // w, x, cols), ("parts", "w", "z", "x", "col"))
    split = ("parts", "w", "z", "x", "col")
    return jax.shard_map(
        shards,
        mesh=mesh,
        in_specs=(
            P(None, split),
            P(split, None, None),
            P(split, None, None),
            P(split, None),
            P(split, None),
            P(split, None),
            P(split, None),
            P(split, None),
            P(split, None),
        ),
        out_specs=P(None, split),
        check_vma=False,
    )
```

```python
import jax
import jax.numpy as jnp
from jax import lax
from jax.experimental import pallas as pl
from jax.experimental.pallas import tpu as pltpu
from jax.sharding import Mesh, PartitionSpec as P

f32 = jnp.float32
bf16 = jnp.bfloat16
LAST = (((1,), (1,)), ((), ()))
PLAIN = (((1,), (0,)), ((), ()))
FIRST = (((0,), (0,)), ((), ()))
HBM = pl.BlockSpec(memory_space=pltpu.HBM)
VMEM = pl.BlockSpec(memory_space=pltpu.VMEM)
EARLY, LATER = 1, 1
UNROLL = 48
GROUP = ("x", "col", "z")


def dot(left, right, dims):
    return lax.dot_general(left, right, dims, preferred_element_type=f32)


def halves(value):
    high = value.astype(bf16)
    return high, (value - high.astype(f32)).astype(bf16)


def one_hot(match):
    return match.astype(f32).astype(bf16)


def side_mask(sides, rank):
    row = lax.broadcasted_iota(jnp.int32, (sides, sides * rank), 0)
    lane = lax.broadcasted_iota(jnp.int32, (sides, sides * rank), 1)
    return lane // rank == row


def start(source, target, sem, priority=0):
    copy = pltpu.make_async_copy(source, target, sem)
    copy.start(priority=priority)
    return copy


def in_hbm(array):
    return pltpu.with_memory_space_constraint(array, pltpu.HBM)


def slot_of(cluster, inner):
    depth, width = inner
    device = cluster >> 1
    return lax.rem(device, 2 * width) * depth + lax.div(device, 2 * width)


def each(count, body):
    if count <= 16:
        for d in range(count):
            body(d)
    else:
        pl.loop(0, count)(body)


def pack_kernel(
    cells_hbm, basis_hbm, first_hbm, second_hbm, coupling_hbm, blocks_hbm,
    out_hbm, mine_ref, far_ref, coupling_ref, early_ref,
    cells_ref, basis_ref, out_ref, sems, *, inner,
):
    copies = [
        start(cells_hbm, cells_ref, sems.at[0]),
        start(basis_hbm, basis_ref, sems.at[1]),
    ]
    ahead = [
        start(first_hbm, far_ref.at[0], sems.at[2]),
        start(second_hbm, far_ref.at[1], sems.at[3]),
        start(coupling_hbm, coupling_ref, sems.at[4], 1),
        start(blocks_hbm.at[pl.ds(0, early_ref.shape[0])], early_ref, sems.at[5], 1),
    ]
    sides = cells_ref.shape[0]
    owned, rank, width = basis_ref.shape
    mask = side_mask(sides, rank)
    for copy in copies:
        copy.wait()
    mine_ref[...] = cells_ref[...]
    blocks, lines = [], []
    for k in range(owned):
        cells = cells_ref[:, k * width : (k + 1) * width]
        blocks.append(cells.astype(f32))
        tiled = jnp.concatenate([basis_ref[k]] * sides, axis=0)
        every = dot(cells, tiled, LAST)
        flat = jnp.sum(jnp.where(mask, every, 0.0), axis=0, keepdims=True)
        lines += [flat[:, :128], flat[:, 128:]]
    moments = jnp.concatenate(lines, axis=0)
    high = moments.astype(bf16).astype(f32)
    moments = jnp.concatenate([high, moments - high], axis=0).astype(bf16)
    for c in range(2):
        half = jnp.concatenate([block[4 * c : 4 * c + 4] for block in blocks], axis=0).astype(bf16)
        for x in range(inner[1]):

            def store(z, c=c, x=x, half=half):
                d = (2 * x + c) * inner[0] + z
                out_ref[d, 0] = half
                out_ref[d, 1] = moments

            each(inner[0], store)
    start(out_ref, out_hbm, sems.at[0]).wait()
    for copy in ahead:
        copy.wait()


def start_indices(owner_hbm, col_hbm, row_hbm, owner, col, row, sems):
    return [
        start(owner_hbm, owner, sems.at[0]),
        start(col_hbm, col, sems.at[1]),
        start(row_hbm, row, sems.at[2]),
    ]


def near_copies(blocks_hbm, first, blocks_ref, chunks, sems):
    size = blocks_ref.shape[0] // chunks
    return [
        start(blocks_hbm.at[pl.ds(first + c * size, size)], blocks_ref.at[pl.ds(c * size, size)], sems.at[3 + c])
        for c in range(chunks)
    ]


def near_loop(first, size, body):
    unroll = min(UNROLL, size)

    def group(g, _):
        body([first + g * unroll + u for u in range(unroll)])
        return 0

    lax.fori_loop(0, size // unroll, group, 0)


def turn_kernel(
    far, coupling_ref, by_row_ref, by_col_ref, gather_ref, spread_ref, *, inner
):
    count, size = coupling_ref.shape
    rank = round(size**0.5)
    devices = gather_ref.shape[0] // 8
    source = lax.broadcasted_iota(jnp.int32, (8 * devices, count), 0)
    target = lax.broadcasted_iota(jnp.int32, (4 * devices, count), 0)
    for n in range(2):
        c = far[n]
        slot, k = slot_of(c, inner), c & 1
        for h in range(2):
            at = 8 * slot + 2 * k + h
            hot = one_hot((source == at) | (source == at + 4))
            gather_ref[:, (2 * n + h) * count : (2 * n + h + 1) * count] = hot
        at = 4 * slot + 2 * k
        hot = ((target == at) | (target == at + 1)).astype(f32).T.astype(bf16)
        spread_ref[2 * n * count : (2 * n + 1) * count, :] = hot
        spread_ref[(2 * n + 1) * count : (2 * n + 2) * count, :] = hot

    for t in range(0, size, 128):
        by_row_ref[t : t + 128, :] = coupling_ref[:, t : t + 128].astype(f32).T
    for k in range(rank):
        by_col_ref[k * rank : (k + 1) * rank, :] = by_row_ref[pl.ds(k, rank, stride=rank), :]


def mirror_kernel(
    owner_hbm, col_hbm, row_hbm, blocks_hbm, early_ref, mine_ref, other_ref,
    keep_ref, give_ref,
    owner, col, row, later_ref, cells_ref, sums_ref, sems, *, inner,
):
    early, width, _ = early_ref.shape
    chunk = early // EARLY
    indices = start_indices(owner_hbm, col_hbm, row_hbm, owner, col, row, sems)
    copies = near_copies(blocks_hbm, early, later_ref, LATER, sems)
    devices = keep_ref.shape[0]
    row_clusters = cells_ref.shape[0]
    me = lax.axis_index("col")
    for k in range(2):
        cells_ref[2 * me + k] = mine_ref[:, k * width : (k + 1) * width].astype(f32)
        cells_ref[2 - 2 * me + k] = other_ref[:, k * width : (k + 1) * width].astype(f32)
    sums_ref[...] = jnp.zeros(sums_ref.shape, f32)

    def multiply(source_ref, first):
        def body(group):
            done = []
            for p in group:
                j = owner[0, p] * row_clusters + col[0, p]
                at = 2 * slot_of(j, inner) + (j & 1)
                cells = cells_ref[row[0, p]].astype(bf16)
                done.append((at, dot(cells, source_ref[p - first], PLAIN)))
            for at, mirrored in done:
                sums_ref[at] += mirrored

        return body

    for copy in indices:
        copy.wait()
    near_loop(0, early, multiply(early_ref, 0))
    for c, copy in enumerate(copies):
        copy.wait()
        near_loop(early + c * chunk, chunk, multiply(later_ref, early))

    def store(d):
        for k in range(2):
            keep_ref[d, k] = sums_ref[2 * d + k, pl.ds(4 * me, 4), :]
            give_ref[d, k] = sums_ref[2 * d + k, pl.ds(4 - 4 * me, 4), :]

    each(devices, store)


def far_kernel(
    every_ref, gather_ref, spread_ref, by_row_ref, by_col_ref,
    far_ref, left_ref, right_ref, lines_ref,
):
    devices = every_ref.shape[0]
    size, count = left_ref.shape
    sides = 8
    rank = size // sides

    lines = every_ref[:, 1].astype(f32).reshape(8 * devices, 128).astype(bf16)
    moments = dot(lines, gather_ref[...], FIRST)
    for h in range(2):
        left_ref[h * 128 : (h + 1) * 128, :] = moments[:, h * count : (h + 1) * count]
        right_ref[h * 128 : (h + 1) * 128, :] = moments[:, (2 + h) * count : (3 + h) * count]

    lines = []
    for h in range(2):
        total = 0.0
        for n, (matrix_ref, source_ref) in enumerate(((by_col_ref, right_ref), (by_row_ref, left_ref))):
            sums = [jnp.zeros((rank, count), f32) for _ in range(sides // 2)]
            for r in range(rank):
                matrix = matrix_ref[r * rank : (r + 1) * rank, :]
                for s in range(sides // 2):
                    at = h * 128 + s * rank + r
                    sums[s] = sums[s] + source_ref[at : at + 1, :] * matrix
            pair = jnp.concatenate(halves(jnp.concatenate(sums, axis=0)), axis=1)
            total = total + dot(pair, spread_ref[2 * n * count : (2 * n + 2) * count, :], PLAIN)
        lines.append(total)
    odd = lax.broadcasted_iota(jnp.int32, (128, 4 * devices), 1) % 2 == 1
    lines_ref[...] = jnp.where(odd, lines[1], lines[0]).T

    def store(d):
        far_ref[d, 0] = lines_ref[pl.ds(4 * d, 4), :]

    each(devices, store)

def join_kernel(far_ref, keep_ref, got_ref, out_hbm, near_ref, sems):
    far = start(far_ref, out_hbm.at[:, pl.ds(2, 1)], sems.at[0])
    near_ref[...] = keep_ref[...] + got_ref[...]
    near = start(near_ref, out_hbm.at[:, pl.ds(0, 2)], sems.at[1])
    far.wait()
    near.wait()


def direct_kernel(
    owner_hbm, col_hbm, row_hbm, blocks_hbm, every_ref, others_ref,
    out_ref, owner, col, row, blocks_ref, cells_ref, sems, *, inner,
):
    indices = start_indices(owner_hbm, col_hbm, row_hbm, owner, col, row, sems)
    copies = near_copies(blocks_hbm, 0, blocks_ref, EARLY + LATER, sems)
    chunk = blocks_ref.shape[0] // (EARLY + LATER)
    row_clusters = out_ref.shape[0]
    out_ref[...] = jnp.zeros(out_ref.shape, f32)
    me = lax.axis_index("col")

    def load(d):
        mine, other = every_ref[d, 0].astype(f32), others_ref[d, 0].astype(f32)
        first, second = jnp.where(me == 0, mine, other), jnp.where(me == 0, other, mine)
        for k in range(2):
            cells_ref[d, k] = jnp.concatenate([first[4 * k : 4 * k + 4], second[4 * k : 4 * k + 4]], axis=0)

    each(every_ref.shape[0], load)
    for copy in indices:
        copy.wait()

    def body(group):
        done = []
        for p in group:
            j = owner[0, p] * row_clusters + col[0, p]
            cells = cells_ref[slot_of(j, inner), j & 1].astype(bf16)
            done.append((row[0, p], dot(cells, blocks_ref[p], LAST)))
        for i, direct in done:
            out_ref[i] += direct

    for c, copy in enumerate(copies):
        copy.wait()
        near_loop(c * chunk, chunk, body)


def finish_kernel(parts_ref, mine_ref, other_ref, basis_ref, out_ref, *, inner):
    owned, rank, width = basis_ref.shape
    sides = out_ref.shape[0]
    depth = inner[0]
    near, far = [], jnp.zeros((4, 128), f32)
    for c in range(2):
        totals = (jnp.zeros((4, 128), f32), jnp.zeros((4, 128), f32), far)
        for x in range(inner[1]):

            def add(z, totals, first=(2 * x + c) * depth):
                return tuple(total + parts_ref[first + z, b] for b, total in enumerate(totals))

            totals = lax.fori_loop(0, depth, add, totals, unroll=min(8, depth))
        near.append(totals[:2])
        far = totals[2]
    me = lax.axis_index("col")
    mask = side_mask(sides, rank)
    for k in range(owned):
        total = jnp.concatenate([near[0][k], near[1][k]], axis=0)
        total = total + (mine_ref[2 * me + k] + other_ref[2 * me + k])
        flat = jnp.concatenate([far[2 * k : 2 * k + 1], far[2 * k + 1 : 2 * k + 2]], axis=1)
        high, low = halves(jnp.where(mask, flat, 0.0))
        tiled = jnp.concatenate([basis_ref[k]] * sides, axis=0)
        total = total + (dot(high, tiled, PLAIN) + dot(low, tiled, PLAIN))
        out_ref[:, k * width : (k + 1) * width] = total


def shards(cells, basis_t, near_blocks, near_owner, near_col, near_row, far_row, far_col, coupling):
    depth = lax.axis_size("z")
    inner = (depth, lax.axis_size("x"))
    devices = 2 * depth * inner[1]
    sides, lanes = cells.shape
    owned, rank, width = basis_t.shape
    row_clusters = owned * lax.axis_size("col")
    pairs = near_blocks.shape[0]
    count = coupling.shape[0]
    swap = [(0, 1), (1, 0)]
    params = pltpu.CompilerParams(vmem_limit_bytes=24 * 1024 * 1024)

    def shaped(shape, dtype):
        return jax.ShapeDtypeStruct(shape, dtype)

    def exchange(blocks):
        return lax.all_to_all(blocks, GROUP, split_axis=0, concat_axis=0, tiled=True)

    turn_cost = pl.CostEstimate(flops=10**6, bytes_accessed=3 * 10**6, transcendentals=0)
    near_cost = pl.CostEstimate(
        flops=2 * pairs * sides * width * width, bytes_accessed=10**7, transcendentals=0
    )
    payload = shaped((devices, 2, sides, 128), bf16)
    owner, column, line = [in_hbm(a.reshape(1, pairs)) for a in (near_owner, near_col, near_row)]
    first, second = [in_hbm(a.reshape(1, count)) for a in (far_row, far_col)]
    blocks = in_hbm(near_blocks)
    part = pairs // (EARLY + LATER)
    block = near_blocks.shape[1:]
    index_scratch = [pltpu.SMEM((1, pairs), jnp.int32)] * 3
    packed, mine, far, couplings, early_blocks = pl.pallas_call(
        lambda *refs: pack_kernel(*refs, inner=inner),
        out_shape=[
            payload,
            shaped(cells.shape, bf16),
            shaped((2, 1, count), jnp.int32),
            shaped(coupling.shape, bf16),
            shaped((EARLY * part,) + block, bf16),
        ],
        in_specs=[HBM] * 6,
        out_specs=[HBM] + [VMEM] * 4,
        scratch_shapes=[
            pltpu.VMEM(cells.shape, bf16),
            pltpu.VMEM(basis_t.shape, bf16),
            pltpu.VMEM(payload.shape, bf16),
            pltpu.SemaphoreType.DMA((6,)),
        ],
        compiler_params=params,
        name="pack",
    )(in_hbm(cells), in_hbm(basis_t), first, second, in_hbm(coupling), blocks)
    every = exchange(packed)
    other = lax.ppermute(mine, "col", swap)
    by_row, by_col, gather, spread = pl.pallas_call(
        lambda *refs: turn_kernel(*refs, inner=inner),
        out_shape=[
            shaped((rank * rank, count), f32),
            shaped((rank * rank, count), f32),
            shaped((8 * devices, 4 * count), bf16),
            shaped((4 * count, 4 * devices), bf16),
        ],
        in_specs=[VMEM] * 2,
        out_specs=[VMEM] * 4,
        compiler_params=params,
        cost_estimate=turn_cost,
        name="turn",
    )(far, couplings)
    keep, give = pl.pallas_call(
        lambda *refs: mirror_kernel(*refs, inner=inner),
        out_shape=[shaped((devices, 2, 4, 128), f32)] * 2,
        in_specs=[HBM] * 4 + [VMEM] * 3,
        out_specs=[VMEM] * 2,
        scratch_shapes=index_scratch
        + [
            pltpu.VMEM((LATER * part,) + block, bf16),
            pltpu.VMEM((row_clusters, sides, width), f32),
            pltpu.VMEM((2 * devices, sides, width), f32),
            pltpu.SemaphoreType.DMA((3 + LATER,)),
        ],
        compiler_params=params,
        cost_estimate=near_cost,
        name="mirror",
    )(owner, column, line, blocks, early_blocks, mine, other)
    got = lax.ppermute(give, "col", swap)
    coupled = pl.pallas_call(
        far_kernel,
        out_shape=shaped((devices, 1, 4, 128), f32),
        in_specs=[VMEM] * 5,
        out_specs=VMEM,
        scratch_shapes=[pltpu.VMEM((sides * rank, count), f32)] * 2 + [pltpu.VMEM((4 * devices, 128), f32)],
        compiler_params=params,
        cost_estimate=turn_cost,
        name="far",
    )(every, gather, spread, by_row, by_col)
    partial = pl.pallas_call(
        join_kernel,
        out_shape=shaped((devices, 3, 4, 128), f32),
        in_specs=[VMEM] * 3,
        out_specs=HBM,
        scratch_shapes=[pltpu.VMEM(keep.shape, f32), pltpu.SemaphoreType.DMA((2,))],
        compiler_params=params,
        name="join",
    )(coupled, keep, got)
    parts = exchange(partial)
    every_other = lax.ppermute(every, "col", swap)
    direct = pl.pallas_call(
        lambda *refs: direct_kernel(*refs, inner=inner),
        out_shape=shaped((row_clusters, sides, width), f32),
        in_specs=[HBM] * 4 + [VMEM] * 2,
        out_specs=VMEM,
        scratch_shapes=index_scratch
        + [
            pltpu.VMEM(near_blocks.shape, bf16),
            pltpu.VMEM(payload.shape, f32),
            pltpu.SemaphoreType.DMA((3 + EARLY + LATER,)),
        ],
        compiler_params=params,
        cost_estimate=near_cost,
        name="direct",
    )(owner, column, line, blocks, every, every_other)
    others = lax.ppermute(direct, "col", swap)
    return pl.pallas_call(
        lambda *refs: finish_kernel(*refs, inner=inner),
        out_shape=shaped((sides, lanes), f32),
        in_specs=[VMEM] * 4,
        out_specs=VMEM,
        compiler_params=params,
        name="finish",
    )(parts, direct, others, basis_t)


def solution(mesh):
    parts, rows, cols = mesh.devices.shape
    x = 2 if rows % 2 == 0 else 1
    mesh = Mesh(mesh.devices.reshape(parts, rows // x, x, cols), ("parts", "z", "x", "col"))
    split = ("parts", "z", "x", "col")
    return jax.shard_map(
        shards,
        mesh=mesh,
        in_specs=(
            P(None, split),
            P(split, None, None),
            P(split, None, None),
            P(split, None),
            P(split, None),
            P(split, None),
            P(split, None),
            P(split, None),
            P(split, None),
        ),
        out_specs=P(None, split),
        check_vma=False,
    )
```
